128 devices in a mesh: blocks: 32 (over z, y, core), loads: 4 (over x).
Axes of the slice: x: 4, y: 4, z: 4, core: 2. Of those that a mesh axis runs over, the one named last changes fastest.
Arguments:
- design: float32 [256, 96, 128], P('blocks'), may hold values from 0.05 to 1
- free_mask: int32 [256, 96, 128], P('blocks'), may hold values 0 or 1
- heat_load: float32 [4, 256, 96, 128], P('loads', 'blocks'), may hold values from -6 to 6
Outputs:
- temperature: float32 [4, 256, 96, 128], P('loads', 'blocks')
- smoothed_objective_slope: float32 [256, 96, 128], P('blocks')
The draws below stay inside these ranges and needn't reach their ends.
Inputs may be any that keep to these rules, and one draw needn't show every extreme that they name: `free_mask`: 1 marks a free cell, 0 a cell held at zero temperature.
All inputs are finite; a program needn't handle non-finite values. No bound on the sum of `free_mask` on one device may be relied on, other than what follows from the above.
Results may differ from the reference program's by a relative error of at most 0.0001.
Values sent between devices are 32-bit elements; how exact they have to be, the bound alone decides.
A program may use at most 128 MiB of HBM per device.

```python
import math
import jax
import jax.numpy as jnp

NY = 96
NZ = 128
ITERS = 2
SWEEPS = 2
LEVELS = 4
LOADS = 4
NX = 256


def place_ends(entries, stream_key, low, largest):
    shape = entries.shape
    place = [jax.random.randint(jax.random.fold_in(stream_key, axis), (), 0, shape[axis]) for axis in range(len(shape))]
    entries = entries.at[tuple(place)].set(low)
    longest = shape.index(max(shape))
    place[longest] = (place[longest] + 1) % shape[longest]
    return entries.at[tuple(place)].set(largest)


def shard_levels(stream_key, dims, split, smallest, largest):
    factor_of, own = 1.0, jax.random.fold_in(stream_key, 6)
    for dim, shards_of in split:
        heights = jnp.exp(jax.random.uniform(jax.random.fold_in(own, dim), (shards_of,), jnp.float32, smallest / len(split), largest / len(split)))
        factor_of = factor_of * jnp.repeat(heights, dims[dim] // shards_of).reshape([-1 if axis == dim else 1 for axis in range(len(dims))])
    return factor_of


def noise(stream_key, shape, scale, limit, cuts=(), kind=jnp.bfloat16):
    array = scale * jax.random.normal(stream_key, shape, jnp.float32)
    if cuts:
        array = array * shard_levels(stream_key, shape, cuts, -0.22, 0.18)
    return jnp.clip(array, -limit, limit).astype(kind)


def setup_inputs(seed: int = 0) -> dict:
    splits = jax.random.split(jax.random.key(seed), 4)
    return {
        "design": jnp.clip(0.05 + 0.95 * jax.random.uniform(splits[0], (NX, NY, NZ), jnp.float32) ** shard_levels(splits[0], (NX, NY, NZ), ((0, 32),), -0.2, 0.2), 0.05, 1.0),
        "free_mask": place_ends((jax.random.randint(splits[1], (NX, NY, NZ), 0, 8) < 7).astype(jnp.int32), jax.random.fold_in(splits[1], 1), 0, 1),
        "heat_load": noise(splits[2], (LOADS, NX, NY, NZ), 1.0, 6.0, ((0, 4), (1, 32)), jnp.float32),
    }


COND_FLOOR = 0.01
PENALTY = 3.0
RELAX_FACTOR = 2.0 / 3.0
HELD_DIAGONAL = 6.0
WEIGHT_CENTER = 1.5
WEIGHT_FACE = 0.5
WEIGHT_EDGE = 1.5 - math.sqrt(2.0)

def pad_sides(values):
    return jnp.pad(values, ((0, 0), (1, 1), (1, 1)))

def pad_ends(values):
    return jnp.pad(values, ((1, 1), (0, 0), (0, 0)))

def blur_padded(bordered_array):
    extent = (bordered_array.shape[0] - 2, bordered_array.shape[1] - 2, bordered_array.shape[2] - 2)

    def shifted(translate_first_axis, shift_y, displaced_depth):
        return bordered_array[1 + translate_first_axis:1 + translate_first_axis + extent[0], 1 + shift_y:1 + shift_y + extent[1], 1 + displaced_depth:1 + displaced_depth + extent[2]]
    face_part = jnp.zeros(extent, jnp.float32)
    edge_part = jnp.zeros(extent, jnp.float32)
    for translate_first_axis in (-1, 0, 1):
        for shift_y in (-1, 0, 1):
            for displaced_depth in (-1, 0, 1):
                reach = abs(translate_first_axis) + abs(shift_y) + abs(displaced_depth)
                if reach == 1:
                    face_part = face_part + shifted(translate_first_axis, shift_y, displaced_depth)
                elif reach == 2:
                    edge_part = edge_part + shifted(translate_first_axis, shift_y, displaced_depth)
    return WEIGHT_CENTER * shifted(0, 0, 0) + WEIGHT_FACE * face_part + WEIGHT_EDGE * edge_part

def face_set(padded_ends, spacing):
    center_cells = padded_ends[1:-1]
    sided = pad_sides(center_cells)
    minus_x = spacing * 0.5 * (center_cells + padded_ends[:-2])
    plus_x = spacing * 0.5 * (center_cells + padded_ends[2:])
    minus_y = spacing * 0.5 * (center_cells + sided[:, :-2, 1:-1])
    plus_y = spacing * 0.5 * (center_cells + sided[:, 2:, 1:-1])
    minus_z = spacing * 0.5 * (center_cells + sided[:, 1:-1, :-2])
    plus_z = spacing * 0.5 * (center_cells + sided[:, 1:-1, 2:])
    plain_diagonal = minus_x + plus_x + minus_y + plus_y + minus_z + plus_z
    return ((minus_x, plus_x, minus_y, plus_y, minus_z, plus_z), plain_diagonal)

def apply_padded(padded_ends, coeffs, plain_diagonal):
    center_cells = padded_ends[1:-1]
    sided = pad_sides(center_cells)
    beside = coeffs[0] * padded_ends[:-2] + coeffs[1] * padded_ends[2:]
    beside = beside + coeffs[2] * sided[:, :-2, 1:-1] + coeffs[3] * sided[:, 2:, 1:-1]
    beside = beside + coeffs[4] * sided[:, 1:-1, :-2] + coeffs[5] * sided[:, 1:-1, 2:]
    return plain_diagonal * center_cells - beside

def face_energy(padded_ends):
    center_cells = padded_ends[1:-1]
    sided = pad_sides(center_cells)
    summed = (center_cells - padded_ends[:-2]) ** 2 + (center_cells - padded_ends[2:]) ** 2
    summed = summed + (center_cells - sided[:, :-2, 1:-1]) ** 2 + (center_cells - sided[:, 2:, 1:-1]) ** 2
    summed = summed + (center_cells - sided[:, 1:-1, :-2]) ** 2 + (center_cells - sided[:, 1:-1, 2:]) ** 2
    return 0.5 * summed

def restrict_sum(values):
    shape_x, shape_y, shape_z = values.shape
    return values.reshape(shape_x // 2, 2, shape_y // 2, 2, shape_z // 2, 2).sum(axis=(1, 3, 5))

def prolong(values):
    shape_x, shape_y, shape_z = values.shape
    spread = jnp.broadcast_to(values[:, None, :, None, :, None], (shape_x, 2, shape_y, 2, shape_z, 2))
    return spread.reshape(2 * shape_x, 2 * shape_y, 2 * shape_z)

def level_apply(values, hierarchy_entries, rim_fn):
    coeffs, plain_diagonal, jacobi, free_share = hierarchy_entries
    if free_share is None:
        return apply_padded(rim_fn(values), coeffs, plain_diagonal)
    masked = free_share * values
    inner_part = apply_padded(rim_fn(masked), coeffs, plain_diagonal)
    return free_share * inner_part + (1.0 - free_share) * HELD_DIAGONAL * values

def smooth_cycle(right_side, start, grades, rim_list):
    hierarchy_entries = grades[start]
    rim_fn = rim_list[start]
    jacobi = hierarchy_entries[2]
    iterate = RELAX_FACTOR * right_side / jacobi
    for sweep_count in range(SWEEPS - 1):
        iterate = iterate + RELAX_FACTOR * (right_side - level_apply(iterate, hierarchy_entries, rim_fn)) / jacobi
    if start + 1 < len(grades):
        equation_mismatch = right_side - level_apply(iterate, hierarchy_entries, rim_fn)
        correction = smooth_cycle(0.5 * restrict_sum(equation_mismatch), start + 1, grades, rim_list)
        iterate = iterate + prolong(correction)
    for sweep_count in range(SWEEPS):
        iterate = iterate + RELAX_FACTOR * (right_side - level_apply(iterate, hierarchy_entries, rim_fn)) / jacobi
    return iterate

def solve_case(scenario_heating, free_share, grades, rim_list, precondition, inner_fn):
    right_side = free_share * scenario_heating
    answer_vector = jnp.zeros_like(right_side)
    mismatch_vector = right_side
    precond = precondition(mismatch_vector)
    direction = precond
    inner_now = inner_fn(mismatch_vector, precond)
    for iteration in range(ITERS):
        product_image = level_apply(direction, grades[0], rim_list[0])
        step_length = inner_now / inner_fn(direction, product_image)
        answer_vector = answer_vector + step_length * direction
        mismatch_vector = mismatch_vector - step_length * product_image
        if iteration + 1 < ITERS:
            precond = precondition(mismatch_vector)
            inner_next = inner_fn(mismatch_vector, precond)
            direction = precond + inner_next / inner_now * direction
            inner_now = inner_next
    return answer_vector

def simple_inner_product(first_vec, second_vec):
    return jnp.sum(first_vec * second_vec)

def reference(design, free_mask, heat_load):
    weight_total = blur_padded(jnp.pad(jnp.ones_like(design), 1))
    density = blur_padded(jnp.pad(design, 1)) / weight_total
    conduct = COND_FLOOR + (1.0 - COND_FLOOR) * density ** PENALTY
    free_share = free_mask.astype(jnp.float32)
    grades = []
    rim_list = []
    current = conduct
    spacing = 1.0
    for number in range(LEVELS):
        coeffs, plain_diagonal = face_set(pad_ends(current), spacing)
        rim_list.append(pad_ends)
        if number == 0:
            grades.append((coeffs, plain_diagonal, free_share * plain_diagonal + (1.0 - free_share) * HELD_DIAGONAL, free_share))
        else:
            grades.append((coeffs, plain_diagonal, plain_diagonal, None))
        if number + 1 < LEVELS:
            current = 0.125 * restrict_sum(current)
            spacing = 2.0 * spacing

    def precondition(mismatch_vector):
        return smooth_cycle(mismatch_vector, 0, grades, rim_list)
    vertex_heat_state = []
    energy = jnp.zeros_like(design)
    for case_id in range(LOADS):
        answer_vector = solve_case(heat_load[case_id], free_share, grades, rim_list, precondition, simple_inner_product)
        vertex_heat_state.append(answer_vector)
        energy = energy + face_energy(pad_ends(free_share * answer_vector))
    gradient = -PENALTY * (1.0 - COND_FLOOR) * density ** (PENALTY - 1.0) * energy
    smoothed_objective_slope = blur_padded(jnp.pad(gradient / weight_total, 1))
    return (jnp.stack(vertex_heat_state), smoothed_objective_slope)
```

```python
import math

import jax
import jax.numpy as jnp
from jax import lax
from jax.experimental import pallas as pl
from jax.experimental.pallas import tpu as pltpu
from jax.sharding import PartitionSpec as P

F32 = jnp.float32
BF16 = jnp.bfloat16
MESH = pl.DeviceIdType.MESH
EDGE = 1.5 - math.sqrt(2.0)
THIRD = 1.0 / 3.0
RELAX = 2.0 / 3.0
NB = 32
NLOAD = 4
ROWS = 96
OWN = 8
REACH = 6
WIN = 2 * REACH + 1


def up_y(v):
    return pltpu.roll(v, v.shape[0] - 1, 0)


def dn_y(v):
    return pltpu.roll(v, 1, 0)


def up_z(v):
    return pltpu.roll(v, 127, 1)


def dn_z(v):
    return pltpu.roll(v, 1, 1)


def lanes(shape):
    return lax.broadcasted_iota(jnp.int32, shape, len(shape) - 1)


def rows_of(shape):
    return lax.broadcasted_iota(jnp.int32, shape, len(shape) - 2)


def exact_dot(x, m):
    hi = x.astype(BF16)
    rest = x - hi.astype(F32)
    mid = rest.astype(BF16)
    low = (rest - mid.astype(F32)).astype(BF16)
    d = lambda a: jnp.dot(a, m, preferred_element_type=F32)
    return d(hi) + d(mid) + d(low)


def stencil(x, xm, xp, cxm, cx, cy, cz):
    s = cx * xp + cxm * xm
    s = s + (cy * up_y(x) + dn_y(cy * x))
    return s + (cz * up_z(x) + dn_z(cz * x))


def loop(a, b, fn, u=0):
    n = b - a
    u = u or next(k for k in (4, 3, 2) if n % k == 0)
    assert n % u == 0

    def step(i, c):
        for k in range(u):
            fn(a + i * u + k)
        return c

    lax.fori_loop(0, n // u, step, 0)


def fold(v):
    return v.reshape(v.shape[0] // 8, 8, 128).sum(axis=0)


def z_sum(f):
    lane = lanes(f.shape)
    return jnp.where(lane == 0, 0.0, dn_z(f)) + jnp.where(lane == 127, 0.0, up_z(f))


def y_sum(f):
    row = rows_of(f.shape)
    last = f.shape[0] - 1
    return jnp.where(row == 0, 0.0, dn_y(f)) + jnp.where(row == last, 0.0, up_y(f))


def blur(f, s):
    h = 0.5 * f + EDGE * s
    zf = z_sum(f)
    return 1.5 * f + 0.5 * s + z_sum(h) + y_sum(h + EDGE * zf)


def kernel(design, mask, heat, temp_out, slope_out, D, MK, HT, COND, CX, CY, CZ, G, J, X, Y, B0, Z0, Q0,
           VA, VB, EA, EB, EC, W0, W1, DW, T0, PT0, C1, CX1, CY1, CZ1, G1, J1, X1, Y1, B1, T1, PT1, CP, CR, BP, BR,
           MP, MR, C2, MC, R, MG, CXU2, CXD2, CY2, CZ2, G2, J2, X2, T3, CX3, CY3, CZ3, G3, J3, PT2,
           AR, EN, RS, GB, TOZ1, TOZ2A, TOZ2B, TOZ3, FRZ1, FRZ2A, FRZ2B, FRZ3, lsem, ssem, rsem):
    me = lax.axis_index("blocks")
    mx = lax.axis_index("loads")

    def block(o):
        return {"blocks": lax.rem(me + o + NB, NB)}

    def load(o):
        return {"loads": lax.rem(mx + o, NLOAD)}

    local = [
        pltpu.make_async_copy(design, D.at[pl.ds(8, 8)], lsem.at[0]),
        pltpu.make_async_copy(mask, MK.at[pl.ds(8, 8)], lsem.at[1]),
        pltpu.make_async_copy(heat.at[0], HT.at[pl.ds(8, 8)], lsem.at[2]),
    ]
    for c in local:
        c.start()

    barrier = pltpu.get_barrier_semaphore()

    def greet(o, c):
        pl.semaphore_signal(barrier, inc=1, device_id=block(o), device_id_type=MESH)
        return c

    lax.fori_loop(1, NB, greet, 0)
    for o in range(1, NLOAD):
        for device in (load(o), {**block(1), **load(o)}, {**block(-1), **load(o)}):
            pl.semaphore_signal(barrier, inc=1, device_id=device, device_id_type=MESH)

    def joined(l, first=7, last=15):
        ends = ((me == 0) & (l == first)) | ((me == NB - 1) & (l == last))
        return jnp.where(ends, 0.0, 1.0).astype(F32)

    def density(l):
        md, mu = joined(l - 1), joined(l)
        weight = W0[...] + (md + mu) * W1[...]
        return blur(D[l], md * D[l - 1] + mu * D[l + 1]) / weight, weight

    def conduct(l):
        d, _ = density(l)
        COND[l] = 0.01 + 0.99 * (d * d * d)

    for c in local:
        c.wait()
    pl.semaphore_wait(barrier, NB - 1 + 3 * (NLOAD - 1))

    sent = []
    count = [0]

    def together(copies, size):
        k = count[0]
        count[0] += 1
        for src, dst, device in copies:
            pltpu.make_async_remote_copy(
                src_ref=src, dst_ref=dst, send_sem=ssem.at[k], recv_sem=rsem.at[k], device_id=device, device_id_type=MESH
            ).start()
        c = pltpu.make_async_remote_copy(
            src_ref=size, dst_ref=size, send_sem=ssem.at[k], recv_sem=rsem.at[k], device_id=block(1), device_id_type=MESH
        )
        sent.append(c)
        return c

    def rim(ref, a, b):
        n = b - a
        return [
            (ref.at[pl.ds(a + 8, n)], ref.at[pl.ds(a, n)], block(1)),
            (ref.at[pl.ds(16 - b, n)], ref.at[pl.ds(24 - b, n)], block(-1)),
        ]

    def layers(n):
        return D.at[pl.ds(0, n)]

    def gather(msg, buf):
        buf[REACH] = msg[...]
        offsets = [s for o in range(1, REACH + 1) for s in (o, -o)]
        return together([(msg, buf.at[REACH - s], block(s)) for s in offsets], buf.at[pl.ds(0, WIN - 1)])

    def reduce_start(values, buf):
        k = count[0]
        count[0] += 1
        lane = lanes((1, 128))
        row = jnp.zeros((1, 128), F32)
        for i, v in enumerate(values):
            row = jnp.where(lane == i, jnp.sum(v), row)
        buf[me] = row

        def send(i, c):
            o = i
            pltpu.make_async_remote_copy(
                src_ref=buf.at[me], dst_ref=buf.at[me], send_sem=ssem.at[k], recv_sem=rsem.at[k],
                device_id=block(o), device_id_type=MESH,
            ).start()
            return c

        lax.fori_loop(1, NB, send, 0)
        c = pltpu.make_async_remote_copy(
            src_ref=buf.at[pl.ds(0, NB - 1)], dst_ref=buf.at[pl.ds(0, NB - 1)], send_sem=ssem.at[k],
            recv_sem=rsem.at[k], device_id=block(1), device_id_type=MESH,
        )
        sent.append(c)
        return c

    def reduce_done(c, buf, n):
        c.wait_recv()
        total = jnp.sum(buf[...], axis=0)
        return [total[:, i : i + 1] for i in range(n)]

    e_design = together(rim(D, 4, 8), layers(8))
    e_mask = together(rim(MK, 5, 8), layers(6))
    e_heat = together(rim(HT, 6, 8), layers(4))

    ii = lax.broadcasted_iota(jnp.int32, (128, 128), 0)
    jj = lax.broadcasted_iota(jnp.int32, (128, 128), 1)
    half_i = lax.shift_right_logical(ii, 1)
    half_j = lax.shift_right_logical(jj, 1)
    put = lambda ref, cond: ref.__setitem__(Ellipsis, jnp.where(cond, 1.0, 0.0).astype(BF16))
    put(TOZ1, half_i == jj)
    put(TOZ2A, (half_i == jj) & (ii < 64))
    put(TOZ2B, (half_i + 32 == jj) & (ii < 64))
    put(TOZ3, (lax.shift_right_logical(ii & 31, 1) == jj) & (ii < 64))
    put(FRZ1, half_j == ii)
    put(FRZ2A, (half_j == ii) & (jj < 64))
    put(FRZ2B, (half_j + 32 == ii) & (jj < 64))
    put(FRZ3, (lax.shift_right_logical(jj & 31, 1) == ii) & (jj < 64))
    plane = (ROWS, 128)
    lane0, row0 = lanes(plane), rows_of(plane)
    one = lambda cond: jnp.where(cond, 1.0, 0.0)
    nz = 2.0 - one(lane0 == 0) - one(lane0 == 127)
    ny = 2.0 - one(row0 == 0) - one(row0 == ROWS - 1)
    W0[...] = 1.5 + 0.5 * (ny + nz) + EDGE * (ny * nz)
    W1[...] = 0.5 + EDGE * (ny + nz)
    T3[pl.ds(312, 8), :] = jnp.zeros((8, 128), F32)
    COND[0] = jnp.zeros(plane, F32)


    def free(l):
        return MK[l].astype(F32)

    def faces(l):
        c = COND[l]
        md, mu = joined(l - 1), joined(l)
        f = free(l)
        cp = COND[l + 1]
        last_row, last_lane = rows_of(plane) == ROWS - 1, lanes(plane) == 127
        first_row, first_lane = rows_of(plane) == 0, lanes(plane) == 0
        cyp = jnp.where(last_row, 0.0, up_y(c))
        czp = jnp.where(last_lane, 0.0, up_z(c))
        cym = jnp.where(first_row, 0.0, dn_y(c))
        czm = jnp.where(first_lane, 0.0, dn_z(c))
        CX[l] = (0.5 * mu) * (c + cp) * (f * free(l + 1))
        CY[l] = jnp.where(last_row, 0.0, 0.5 * (c + cyp) * (f * up_y(f)))
        CZ[l] = jnp.where(last_lane, 0.0, 0.5 * (c + czp) * (f * up_z(f)))
        diag = 3.0 * c + 0.5 * (mu * cp + md * COND[l - 1] + (cyp + cym) + (czp + czm))
        j = f * diag + (1.0 - f) * 6.0
        J[l] = j
        G[l] = RELAX / j

    def right_side(l):
        b = free(l) * HT[l]
        B0[l] = b
        X[l] = G[l] * b

    loop(9, 15, conduct)
    loop(10, 14, faces)
    loop(10, 14, right_side)
    e_design.wait_recv()
    loop(5, 9, conduct)
    loop(15, 19, conduct)

    def pair_z1(n, scale):
        rows = T0[pl.ds(0, n * 48, 2), :] + T0[pl.ds(1, n * 48, 2), :]
        return (exact_dot(rows, TOZ1[...]) * scale).reshape(n, 48, 128)

    def pair_cond(i):
        T0[pl.ds(pl.multiple_of(i * 96, 8), 96), :] = COND[8 + 2 * i] + COND[9 + 2 * i]

    loop(0, 4, pair_cond)
    C1[pl.ds(4, 4)] = pair_z1(4, 0.125)
    CP[0] = C1[4] + pltpu.roll(C1[5], 64, 1)
    CP[1] = C1[6] + pltpu.roll(C1[7], 64, 1)
    e_cond = together([(CP, CR.at[0], block(1)), (CP, CR.at[1], block(-1))], CR)

    def pair_z2(src, msg, scale):
        for i in range(2):
            T1[pl.ds(48 * i, 48), :] = src(2 * i) + src(2 * i + 1)
        rows = T1[pl.ds(0, 48, 2), :] + T1[pl.ds(1, 48, 2), :]
        msg[...] = (exact_dot(rows[:24], TOZ2A[...]) + exact_dot(rows[24:], TOZ2B[...])) * scale


    e_mask.wait_recv()
    loop(6, 10, faces)
    loop(14, 18, faces)
    e_heat.wait_recv()
    loop(6, 10, right_side)
    loop(14, 18, right_side)

    def apply0(ref, l):
        return stencil(ref[l], ref[l - 1], ref[l + 1], CX[l - 1], CX[l], CY[l], CZ[l])

    def sweep0(src, dst, b):
        def one_layer(l):
            dst[l] = src[l] * THIRD + G[l] * (b[l] + apply0(src, l))

        return one_layer

    def residual0(src, b, first):
        def pair(i):
            total = None
            for k in range(2):
                l = first + 2 * i + k
                r = b[l] - J[l] * src[l] + apply0(src, l)
                total = r if total is None else total + r
            T0[pl.ds(pl.multiple_of(i * 96, 8), 96), :] = total

        return pair

    def apply1(ref, l):
        return stencil(ref[l], ref[l - 1], ref[l + 1], CX1[l - 1], CX1[l], CY1[l], CZ1[l])

    def sweep1(src, dst):
        def one_layer(l):
            dst[l] = src[l] * THIRD + G1[l] * (B1[l] + apply1(src, l))

        return one_layer

    def faces1():
        shape = (48, 128)
        lane, row = lanes(shape), rows_of(shape)
        for side, base in ((0, 0), (1, 8)):
            for i in range(2):
                v = CR[side, i]
                C1[base + 2 * i] = jnp.where(lane < 64, v, 0.0)
                C1[base + 2 * i + 1] = jnp.where(lane < 64, pltpu.roll(v, 64, 1), 0.0)
        CX1[0] = C1[0] + C1[1]

        def one_layer(l):
            c = C1[l]
            md, mu = joined(l - 1, 3, 7), joined(l, 3, 7)
            cp = C1[l + 1]
            cyp = jnp.where(row == 47, 0.0, up_y(c))
            czp = up_z(c)
            cym = jnp.where(row == 0, 0.0, dn_y(c))
            czm = dn_z(c)
            CX1[l] = mu * (c + cp)
            CY1[l] = jnp.where(row == 47, 0.0, c + cyp)
            CZ1[l] = jnp.where(lane >= 63, 0.0, c + czp)
            diag = 6.0 * c + (mu * cp + md * C1[l - 1] + (cyp + cym) + (czp + czm))
            j = jnp.where(lane < 64, diag, 1.0)
            J1[l] = j
            G1[l] = RELAX / j

        loop(1, 11, one_layer)

    def level1_down(msg, packed):
        def start(l):
            X1[l] = G1[l] * B1[l]

        loop(2, 10, start, 4)
        loop(3, 9, sweep1(X1, Y1))
        for l in range(4):
            packed[l] = Y1[4 + l] + pltpu.roll(B1[4 + l], 64, 1)

        def mismatch(i):
            l = 4 + i
            return B1[l] - J1[l] * Y1[l] + apply1(Y1, l)

        pair_z2(mismatch, msg, 0.5)

    def level1_up(recv, a):
        for side, base in ((0, 0), (1, 8)):
            for i in range(4):
                v = recv[side, i]
                Y1[base + i] = v
                B1[base + i] = pltpu.roll(v, 64, 1)
        for l in range(a, 12 - a):
            X1[l] = Y1[l] + PT1[(l % 4) // 2, pl.ds(48 * (l // 4), 48), :]
        loop(a + 1, 11 - a, sweep1(X1, Y1))
        loop(a + 2, 10 - a, sweep1(Y1, X1))

    wide = (WIN * 24, 128)
    lane2 = lanes(wide)
    block2 = lax.broadcasted_iota(jnp.int32, (WIN, 24, 128), 0).reshape(wide)
    y2 = lax.broadcasted_iota(jnp.int32, (WIN, 24, 128), 1).reshape(wide)
    cut = lax.rem(NB - 1 - me + REACH, NB)

    def around2(v):
        n = v.shape[0]
        lane = lanes(v.shape)
        plus, minus = pltpu.roll(v, 32, 1), pltpu.roll(v, 96, 1)
        above = jnp.where(lane < 32, minus, pltpu.roll(plus, n - 24, 0))
        below = jnp.where(lane < 32, pltpu.roll(minus, 24, 0), plus)
        return above, below

    def faces2():
        c = C2[...].reshape(wide)
        above, below = around2(c)
        low = lane2 < 32
        used = lane2 < 64
        above = jnp.where((block2 == cut) & (lane2 >= 32), 0.0, above)
        below = jnp.where((block2 == cut + 1) & low, 0.0, below)
        cyp = jnp.where(y2 == 23, 0.0, up_y(c))
        cym = jnp.where(y2 == 0, 0.0, dn_y(c))
        zl = lane2 & 31
        czp = jnp.where(zl == 31, 0.0, up_z(c))
        czm = jnp.where(zl == 0, 0.0, dn_z(c))
        cut_up = ((block2 == cut) & (lane2 >= 32)) | (lane2 >= 64)
        cut_down = ((block2 == cut + 1) & low) | (lane2 >= 64)
        CXU2[...] = jnp.where(cut_up, 0.0, 2.0 * (c + above))
        CXD2[...] = jnp.where(cut_down, 0.0, 2.0 * (c + below))
        CY2[...] = jnp.where(y2 == 23, 0.0, 2.0 * (c + cyp))
        CZ2[...] = jnp.where((zl == 31) | (lane2 >= 64), 0.0, 2.0 * (c + czp))
        diag = 12.0 * c + 2.0 * ((above + below) + (cyp + cym) + (czp + czm))
        j = jnp.where(used, diag, 1.0)
        J2[...] = j
        G2[...] = RELAX / j
        T3[pl.ds(0, 312), :] = exact_dot(c, TOZ3[...])
        c3 = (T3[pl.ds(0, 160, 2), :] + T3[pl.ds(1, 160, 2), :]) * 0.125
        shape = (160, 128)
        lane, row = lanes(shape), rows_of(shape)
        blk = lax.shift_right_logical(row * 5462, 16)
        y = row - 12 * blk
        a3 = jnp.where(blk == cut, 0.0, pltpu.roll(c3, 148, 0))
        b3 = jnp.where(blk == cut + 1, 0.0, pltpu.roll(c3, 12, 0))
        yp = jnp.where(y == 11, 0.0, up_y(c3))
        ym = jnp.where(y == 0, 0.0, dn_y(c3))
        zp, zm = up_z(c3), dn_z(c3)
        CX3[...] = jnp.where(blk == cut, 0.0, 4.0 * (c3 + a3))
        CY3[...] = jnp.where(y == 11, 0.0, 4.0 * (c3 + yp))
        CZ3[...] = jnp.where(lane >= 15, 0.0, 4.0 * (c3 + zp))
        diag3 = 24.0 * c3 + 4.0 * ((a3 + b3) + (yp + ym) + (zp + zm))
        j3 = jnp.where((lane < 16) & (row < 156), diag3, 1.0)
        J3[...] = j3
        G3[...] = RELAX / j3

    def apply2(x, part):
        above, below = around2(x)
        cy, cz = CY2[part, :], CZ2[part, :]
        s = CXU2[part, :] * above + CXD2[part, :] * below
        s = s + (cy * up_y(x) + dn_y(cy * x))
        return s + (cz * up_z(x) + dn_z(cz * x))

    def apply3(x):
        cx, cy, cz = CX3[...], CY3[...], CZ3[...]
        s = cx * pltpu.roll(x, 148, 0) + pltpu.roll(cx * x, 12, 0)
        s = s + (cy * up_y(x) + dn_y(cy * x))
        return s + (cz * up_z(x) + dn_z(cz * x))

    def coarse(buf):
        whole = pl.ds(0, WIN * 24)
        b = buf[...].reshape(wide)
        x = G2[...] * b
        x = x * THIRD + G2[...] * (b + apply2(x, whole))
        X2[...] = x
        r = b - J2[...] * x + apply2(x, whole)
        T3[pl.ds(0, 312), :] = exact_dot(r, TOZ3[...])
        b3 = (T3[pl.ds(0, 160, 2), :] + T3[pl.ds(1, 160, 2), :]) * 0.5
        g3 = G3[...]
        x3 = g3 * b3
        for _ in range(3):
            x3 = x3 * THIRD + g3 * (b3 + apply3(x3))
        spread = exact_dot(x3[48:112], FRZ3[...])
        PT2[pl.ds(0, 64, 2), :] = spread
        PT2[pl.ds(1, 64, 2), :] = spread
        part = pl.ds(96, 120)
        b = buf[pl.ds(4, 5)].reshape(120, 128)
        x = X2[part, :] + PT2[pl.ds(0, 120), :]
        g = G2[part, :]
        for _ in range(2):
            x = x * THIRD + g * (b + apply2(x, part))
        x = x[24:96]
        for k, m in enumerate((FRZ2A, FRZ2B)):
            spread = exact_dot(x, m[...])
            PT1[k, pl.ds(0, 72, 2), :] = spread
            PT1[k, pl.ds(1, 72, 2), :] = spread

    def spread0(first, n):
        x = X1[pl.ds(first, n)].reshape(n * 48, 128)
        spread = exact_dot(x, FRZ1[...])
        PT0[pl.ds(0, n * 48, 2), :] = spread
        PT0[pl.ds(1, n * 48, 2), :] = spread

        def add(i):
            p = PT0[pl.ds(pl.multiple_of(i * 96, 8), 96), :]
            l = 2 * (first + i)
            X[l] = Y[l] + p
            X[l + 1] = Y[l + 1] + p

        loop(0, n, add)

    loop(7, 17, sweep0(X, Y, B0))
    loop(0, 4, residual0(Y, B0, 8), 1)
    B1[pl.ds(4, 4)] = pair_z1(4, 0.5)
    BP[0] = B1[4] + pltpu.roll(B1[5], 64, 1)
    BP[1] = B1[6] + pltpu.roll(B1[7], 64, 1)
    e_b1 = together([(BP.at[1], BR.at[0], block(1)), (BP.at[0], BR.at[1], block(-1))], BR)
    pair_z2(lambda i: C1[4 + i], MC, 0.125)
    g_cond = gather(MC, C2)
    e_next = together(rim(D, 3, 4) + rim(MK, 4, 5) + rim(HT, 5, 6), layers(6))
    e_cond.wait_recv()
    faces1()
    e_b1.wait_recv()
    for side, base in ((0, 2), (1, 8)):
        B1[base] = BR[side]
        B1[base + 1] = pltpu.roll(BR[side], 64, 1)
    level1_down(MG.at[0], MP.at[0])
    g_one = gather(MG.at[0], R.at[0])
    e_m1 = together([(MP.at[0], MR.at[0, 0], block(1)), (MP.at[0], MR.at[0, 1], block(-1))], MR.at[0])

    e_rest = together(rim(D, 0, 3) + rim(MK, 1, 4), layers(12))

    g_cond.wait_recv()
    faces2()

    def slope_factor(l):
        d, weight = density(l)
        DW[l - 8] = (-3.0 * 0.99) * (d * d) / weight

    loop(8, 16, slope_factor)
    e_next.wait_recv()
    for l in (4, 19):
        conduct(l)
    for l in (5, 18):
        faces(l)
    for l in (5, 18):
        right_side(l)
    for l in (6, 17):
        sweep0(X, Y, B0)(l)

    g_one.wait_recv()
    coarse(R.at[0])
    e_m1.wait_recv()
    level1_up(MR.at[0], 1)
    spread0(3, 6)
    loop(7, 17, sweep0(X, Y, B0))
    post = sweep0(Y, Z0, B0)
    loop(8, 16, post)
    e_near = together(rim(Z0, 4, 8), layers(8))
    e_far = together(rim(Z0, 1, 4), layers(6))

    def image(l):
        q = J[l] * Z0[l] - apply0(Z0, l)
        Q0[l] = q
        X[l] = G[l] * q

    loop(9, 15, image)
    e_rest.wait_recv()
    loop(1, 4, conduct, 1)
    loop(20, 23, conduct, 1)
    loop(1, 5, faces)
    loop(19, 22, faces, 1)
    e_near.wait_recv()
    loop(5, 9, image)
    loop(15, 19, image)

    def inner0(i, c):
        l = OWN + i
        z = Z0[l]
        return c[0] + fold(B0[l] * z), c[1] + fold(z * Q0[l])

    nil = jnp.zeros((8, 128), F32)
    ar0 = reduce_start(lax.fori_loop(0, 8, inner0, (nil, nil)), AR.at[0])
    pre = sweep0(X, Y, Q0)
    mismatch0 = residual0(Y, Q0, 4)
    loop(6, 18, pre)
    loop(2, 6, mismatch0, 1)
    e_far.wait_recv()
    loop(2, 5, image, 1)
    loop(19, 22, image, 1)
    loop(3, 6, pre, 1)
    loop(18, 21, pre, 1)
    loop(0, 2, mismatch0, 1)
    loop(6, 8, mismatch0, 1)
    B1[pl.ds(2, 8)] = pair_z1(8, 0.5)
    level1_down(MG.at[1], MP.at[1])
    g_two = gather(MG.at[1], R.at[1])
    e_m2 = together([(MP.at[1], MR.at[1, 0], block(1)), (MP.at[1], MR.at[1, 1], block(-1))], MR.at[1])

    def masked(l):
        VA[l] = free(l) * Z0[l]

    loop(7, 17, masked)
    rho0, pq0 = reduce_done(ar0, AR.at[0], 2)
    a0 = rho0 / pq0
    g_two.wait_recv()
    coarse(R.at[1])
    e_m2.wait_recv()
    level1_up(MR.at[1], 0)
    spread0(2, 8)
    loop(6, 18, sweep0(X, Y, Q0))

    def last_sweep(l):
        w = Y[l] * THIRD + G[l] * (Q0[l] + apply0(Y, l))
        z = Z0[l] - a0 * w
        X[l] = z
        VB[l] = free(l) * z

    loop(7, 17, last_sweep)

    def inner1(i, c):
        l = OWN + i
        z = X[l]
        bz = J[l] * z - apply0(X, l)
        q = Q0[l]
        r = B0[l] - a0 * q
        return c[0] + fold(r * z), c[1] + fold(z * bz), c[2] + fold(z * q)

    ar1 = reduce_start(lax.fori_loop(0, 8, inner1, (nil, nil, nil)), AR.at[1])

    def forms(l):
        md, mu = joined(l - 1), joined(l)
        row, lane = rows_of(plane), lanes(plane)
        a, b = VA[l], VB[l]

        def gaps(ref, v):
            return (
                v - md * ref[l - 1],
                v - mu * ref[l + 1],
                v - jnp.where(row == ROWS - 1, 0.0, up_y(v)),
                v - jnp.where(lane == 127, 0.0, up_z(v)),
            )

        ga, gb = gaps(VA, a), gaps(VB, b)

        def form(g, h, vv):
            dy, dz = g[2] * h[2], g[3] * h[3]
            e = g[0] * h[0] + g[1] * h[1] + dy + dz
            return e + jnp.where(row == 0, vv, dn_y(dy)) + jnp.where(lane == 0, vv, dn_z(dz))

        EA[l - 8] = form(ga, ga, a * a)
        EB[l - 8] = form(ga, gb, a * b)
        EC[l - 8] = form(gb, gb, b * b)

    loop(8, 16, forms, 1)
    rho1, zbz, zq = reduce_done(ar1, AR.at[1], 3)
    beta = rho1 / rho0
    pq1 = zbz + 2.0 * beta * zq + beta * beta * pq0
    a1 = rho1 / pq1
    on_z0 = a0 + a1 * beta
    faa, fab, fbb = 0.5 * on_z0 * on_z0, on_z0 * a1, 0.5 * a1 * a1

    def energy(l):
        EN[l] = faa * EA[l] + fab * EB[l] + fbb * EC[l]

    def quarter(x):
        return pl.ds(pl.multiple_of(24 * x, 8), 24)

    mine = quarter(mx)
    pieces = ((0, 3), (3, 6), (6, 8))
    e_energy, e_slope = [], []
    for first, end in pieces:
        loop(first, end, energy, 1)
        part = pl.ds(first, end - first)
        e_energy.append(
            together(
                [
                    (EN.at[part, quarter(lax.rem(mx + o, NLOAD)), :], RS.at[o - 1, part], load(o))
                    for o in range(1, NLOAD)
                ],
                RS.at[:, part],
            )
        )

    def answer(i):
        temp_out[0, i] = on_z0 * Z0[OWN + i] + a1 * X[OWN + i]

    loop(0, 8, answer)

    def total(l):
        e = EN[l, mine, :] + RS[0, l] + RS[1, l] + RS[2, l]
        GB[l + 1, mine, :] = e * DW[l, mine, :]

    for came, (first, end) in zip(e_energy, pieces):
        came.wait_recv()
        loop(first, end, total, end - first)
        copies = []
        for edge, layer, halo, o in ((0, 1, 9, -1), (8, 8, 0, 1)):
            if edge in (first, end):
                copies += [
                    (GB.at[layer, mine, :], GB.at[halo, mine, :], {**block(o), **load(k)}) for k in range(NLOAD)
                ]
        part = GB.at[pl.ds(first + 1, end - first), mine, :]
        size = T0.at[pl.ds(0, 24 * (len(copies) + 3 * (end - first))), :]
        e_slope.append(together(copies + [(part, part, load(o)) for o in range(1, NLOAD)], size))

    def smooth(i):
        s = joined(i + 7) * GB[i] + joined(i + 8) * GB[i + 2]
        slope_out[i] = blur(GB[i + 1], s)

    done_to = 1
    for came, (first, end) in zip(e_slope, pieces):
        came.wait_recv()
        ready = end if end == 8 else end - 1
        loop(done_to, ready, smooth, 1)
        done_to = ready
    smooth(0)
    for c in sent:
        c.wait_send()


def relay(temp, slope, temp_out, slope_out, sem):
    copies = [
        pltpu.make_async_copy(temp, temp_out, sem.at[0]),
        pltpu.make_async_copy(slope, slope_out, sem.at[1]),
    ]
    for c in copies:
        c.start()
    for c in copies:
        c.wait()


def body(design, free_mask, heat_load):
    v = lambda *s: pltpu.VMEM(s, F32)
    brick = v(24, ROWS, 128)
    level1 = v(12, 48, 128)
    level2 = v(WIN * 24, 128)
    level3 = v(160, 128)
    square = pltpu.VMEM((128, 128), BF16)
    scratch = [
        brick, pltpu.VMEM((24, ROWS, 128), jnp.int32), brick,
        brick, brick, brick, brick, brick, brick, brick, brick, brick, brick, brick,
        brick, brick, v(8, ROWS, 128), v(8, ROWS, 128), v(8, ROWS, 128),
        v(ROWS, 128), v(ROWS, 128), v(8, ROWS, 128), v(768, 128), v(768, 128),
        level1, level1, level1, level1, level1, level1, level1, level1, level1,
        v(96, 128), v(2, 144, 128), v(2, 48, 128), v(2, 2, 48, 128), v(2, 48, 128), v(2, 48, 128),
        v(2, 4, 48, 128), v(2, 2, 4, 48, 128), v(WIN, 24, 128), v(24, 128),
        v(2, WIN, 24, 128), v(2, 24, 128),
        level2, level2, level2, level2, level2, level2, level2, v(320, 128),
        level3, level3, level3, level3, level3, v(128, 128),
        v(2, NB, 1, 128), v(8, ROWS, 128), v(3, 8, 24, 128), v(10, ROWS, 128),
        square, square, square, square, square, square, square, square,
        pltpu.SemaphoreType.DMA((3,)), pltpu.SemaphoreType.DMA((22,)), pltpu.SemaphoreType.DMA((22,)),
    ]
    inside = pl.BlockSpec(memory_space=pltpu.VMEM)
    hbm = pl.BlockSpec(memory_space=pltpu.HBM)
    outs = (jax.ShapeDtypeStruct(heat_load.shape, F32), jax.ShapeDtypeStruct(design.shape, F32))
    temp, slope = pl.pallas_call(
        kernel,
        out_shape=(pltpu.VMEM(heat_load.shape, F32), pltpu.VMEM(design.shape, F32)),
        in_specs=[hbm] * 3,
        out_specs=(inside, inside),
        scratch_shapes=scratch,
        compiler_params=pltpu.CompilerParams(
            collective_id=0, has_side_effects=True, vmem_limit_bytes=62 * 2**20
        ),
    )(design, free_mask, heat_load)
    return pl.pallas_call(
        relay,
        out_shape=outs,
        in_specs=[inside] * 2,
        out_specs=(hbm, hbm),
        scratch_shapes=[pltpu.SemaphoreType.DMA((2,))],
        compiler_params=pltpu.CompilerParams(vmem_limit_bytes=4 * 2**20),
    )(temp, slope)


def solution(mesh):
    return jax.shard_map(
        body,
        mesh=mesh,
        in_specs=(P("blocks", None, None), P("blocks", None, None), P("loads", "blocks", None, None)),
        out_specs=(P("loads", "blocks", None, None), P("blocks", None, None)),
        check_vma=False,
    )
```

```python
import math

import jax
import jax.numpy as jnp
from jax import lax
from jax.experimental import pallas as pl
from jax.experimental.pallas import tpu as pltpu
from jax.sharding import PartitionSpec as P

F32 = jnp.float32
BF16 = jnp.bfloat16
MESH = pl.DeviceIdType.MESH
EDGE = 1.5 - math.sqrt(2.0)
THIRD = 1.0 / 3.0
RELAX = 2.0 / 3.0
NB = 32
NLOAD = 4
ROWS = 96
OWN = 8
REACH = 6
WIN = 2 * REACH + 1


def up_y(v):
    return pltpu.roll(v, v.shape[0] - 1, 0)


def dn_y(v):
    return pltpu.roll(v, 1, 0)


def up_z(v):
    return pltpu.roll(v, 127, 1)


def dn_z(v):
    return pltpu.roll(v, 1, 1)


def lanes(shape):
    return lax.broadcasted_iota(jnp.int32, shape, len(shape) - 1)


def rows_of(shape):
    return lax.broadcasted_iota(jnp.int32, shape, len(shape) - 2)


def exact_dot(x, m):
    hi = x.astype(BF16)
    rest = x - hi.astype(F32)
    mid = rest.astype(BF16)
    d = lambda a: jnp.dot(a, m, preferred_element_type=F32)
    return d(hi) + d(mid)


def stencil(x, xm, xp, cxm, cx, cy, cz):
    s = cx * xp + cxm * xm
    s = s + (cy * up_y(x) + dn_y(cy * x))
    return s + (cz * up_z(x) + dn_z(cz * x))


def loop(a, b, fn, u=0):
    n = b - a
    u = u or next(k for k in (4, 3, 2) if n % k == 0)
    assert n % u == 0

    def step(i, c):
        for k in range(u):
            fn(a + i * u + k)
        return c

    lax.fori_loop(0, n // u, step, 0)


def fold(v):
    return v.reshape(v.shape[0] // 8, 8, 128).sum(axis=0)


def z_sum(f):
    lane = lanes(f.shape)
    return jnp.where(lane == 0, 0.0, dn_z(f)) + jnp.where(lane == 127, 0.0, up_z(f))


def y_sum(f):
    row = rows_of(f.shape)
    last = f.shape[0] - 1
    return jnp.where(row == 0, 0.0, dn_y(f)) + jnp.where(row == last, 0.0, up_y(f))


def blur(f, s):
    h = 0.5 * f + EDGE * s
    zf = z_sum(f)
    return 1.5 * f + 0.5 * s + z_sum(h) + y_sum(h + EDGE * zf)


def kernel(design, mask, heat, temp_out, slope_out, D, MK, HT, COND, CX, CY, CZ, G, J, X, Y, B0, Z0, Q0,
           VA, VB, EA, EB, EC, W0, W1, DW, T0, PT0, C1, CX1, CY1, CZ1, G1, J1, X1, Y1, B1, T1, PT1, CP, CR, BP, BR,
           MP, MR, C2, MC, R, MG, CXU2, CXD2, CY2, CZ2, G2, J2, X2, T3, CX3, CY3, CZ3, G3, J3, PT2,
           AR, EN, RS, GB, TOZ1, TOZ2A, TOZ2B, TOZ3, FRZ1, FRZ2A, FRZ2B, FRZ3, lsem, ssem, rsem):
    me = lax.axis_index("blocks")
    mx = lax.axis_index("loads")

    def block(o):
        return {"blocks": lax.rem(me + o + NB, NB)}

    def load(o):
        return {"loads": lax.rem(mx + o, NLOAD)}

    local = [
        pltpu.make_async_copy(design, D.at[pl.ds(8, 8)], lsem.at[0]),
        pltpu.make_async_copy(mask, MK.at[pl.ds(8, 8)], lsem.at[1]),
        pltpu.make_async_copy(heat.at[0], HT.at[pl.ds(8, 8)], lsem.at[2]),
    ]
    for c in local:
        c.start()

    barrier = pltpu.get_barrier_semaphore()

    def greet(o, c):
        pl.semaphore_signal(barrier, inc=1, device_id=block(o), device_id_type=MESH)
        return c

    lax.fori_loop(1, NB, greet, 0)
    for o in range(1, NLOAD):
        for device in (load(o), {**block(1), **load(o)}, {**block(-1), **load(o)}):
            pl.semaphore_signal(barrier, inc=1, device_id=device, device_id_type=MESH)

    def joined(l, first=7, last=15):
        ends = ((me == 0) & (l == first)) | ((me == NB - 1) & (l == last))
        return jnp.where(ends, 0.0, 1.0).astype(F32)

    def density(l):
        md, mu = joined(l - 1), joined(l)
        weight = W0[...] + (md + mu) * W1[...]
        return blur(D[l], md * D[l - 1] + mu * D[l + 1]) / weight, weight

    def conduct(l):
        d, _ = density(l)
        COND[l] = 0.01 + 0.99 * (d * d * d)

    for c in local:
        c.wait()
    pl.semaphore_wait(barrier, NB - 1 + 3 * (NLOAD - 1))

    sent = []
    count = [0]

    def together(copies, size):
        k = count[0]
        count[0] += 1
        for src, dst, device in copies:
            pltpu.make_async_remote_copy(
                src_ref=src, dst_ref=dst, send_sem=ssem.at[k], recv_sem=rsem.at[k], device_id=device, device_id_type=MESH
            ).start()
        c = pltpu.make_async_remote_copy(
            src_ref=size, dst_ref=size, send_sem=ssem.at[k], recv_sem=rsem.at[k], device_id=block(1), device_id_type=MESH
        )
        sent.append(c)
        return c

    def rim(ref, a, b):
        n = b - a
        return [
            (ref.at[pl.ds(a + 8, n)], ref.at[pl.ds(a, n)], block(1)),
            (ref.at[pl.ds(16 - b, n)], ref.at[pl.ds(24 - b, n)], block(-1)),
        ]

    def layers(n):
        return D.at[pl.ds(0, n)]

    def gather(msg, buf):
        buf[REACH] = msg[...]
        offsets = [s for o in range(1, REACH + 1) for s in (o, -o)]
        return together([(msg, buf.at[REACH - s], block(s)) for s in offsets], buf.at[pl.ds(0, WIN - 1)])

    def reduce_start(values, buf):
        k = count[0]
        count[0] += 1
        lane = lanes((1, 128))
        row = jnp.zeros((1, 128), F32)
        for i, v in enumerate(values):
            row = jnp.where(lane == i, jnp.sum(v), row)
        buf[me] = row

        def send(i, c):
            o = i
            pltpu.make_async_remote_copy(
                src_ref=buf.at[me], dst_ref=buf.at[me], send_sem=ssem.at[k], recv_sem=rsem.at[k],
                device_id=block(o), device_id_type=MESH,
            ).start()
            return c

        lax.fori_loop(1, NB, send, 0)
        c = pltpu.make_async_remote_copy(
            src_ref=buf.at[pl.ds(0, NB - 1)], dst_ref=buf.at[pl.ds(0, NB - 1)], send_sem=ssem.at[k],
            recv_sem=rsem.at[k], device_id=block(1), device_id_type=MESH,
        )
        sent.append(c)
        return c

    def reduce_done(c, buf, n):
        c.wait_recv()
        total = jnp.sum(buf[...], axis=0)
        return [total[:, i : i + 1] for i in range(n)]

    e_design = together(rim(D, 4, 8), layers(8))
    e_mask = together(rim(MK, 5, 8), layers(6))
    e_heat = together(rim(HT, 6, 8), layers(4))

    ii = lax.broadcasted_iota(jnp.int32, (128, 128), 0)
    jj = lax.broadcasted_iota(jnp.int32, (128, 128), 1)
    half_i = lax.shift_right_logical(ii, 1)
    half_j = lax.shift_right_logical(jj, 1)
    put = lambda ref, cond: ref.__setitem__(Ellipsis, jnp.where(cond, 1.0, 0.0).astype(BF16))
    put(TOZ1, half_i == jj)
    put(TOZ2A, (half_i == jj) & (ii < 64))
    put(TOZ2B, (half_i + 32 == jj) & (ii < 64))
    put(TOZ3, (lax.shift_right_logical(ii & 31, 1) == jj) & (ii < 64))
    put(FRZ1, half_j == ii)
    put(FRZ2A, (half_j == ii) & (jj < 64))
    put(FRZ2B, (half_j + 32 == ii) & (jj < 64))
    put(FRZ3, (lax.shift_right_logical(jj & 31, 1) == ii) & (jj < 64))
    plane = (ROWS, 128)
    lane0, row0 = lanes(plane), rows_of(plane)
    one = lambda cond: jnp.where(cond, 1.0, 0.0)
    nz = 2.0 - one(lane0 == 0) - one(lane0 == 127)
    ny = 2.0 - one(row0 == 0) - one(row0 == ROWS - 1)
    W0[...] = 1.5 + 0.5 * (ny + nz) + EDGE * (ny * nz)
    W1[...] = 0.5 + EDGE * (ny + nz)
    T3[pl.ds(312, 8), :] = jnp.zeros((8, 128), F32)
    COND[0] = jnp.zeros(plane, F32)


    def free(l):
        return MK[l].astype(F32)

    def faces(l):
        c = COND[l]
        md, mu = joined(l - 1), joined(l)
        f = free(l)
        cp = COND[l + 1]
        last_row, last_lane = rows_of(plane) == ROWS - 1, lanes(plane) == 127
        first_row, first_lane = rows_of(plane) == 0, lanes(plane) == 0
        cyp = jnp.where(last_row, 0.0, up_y(c))
        czp = jnp.where(last_lane, 0.0, up_z(c))
        cym = jnp.where(first_row, 0.0, dn_y(c))
        czm = jnp.where(first_lane, 0.0, dn_z(c))
        CX[l] = (0.5 * mu) * (c + cp) * (f * free(l + 1))
        CY[l] = jnp.where(last_row, 0.0, 0.5 * (c + cyp) * (f * up_y(f)))
        CZ[l] = jnp.where(last_lane, 0.0, 0.5 * (c + czp) * (f * up_z(f)))
        diag = 3.0 * c + 0.5 * (mu * cp + md * COND[l - 1] + (cyp + cym) + (czp + czm))
        j = f * diag + (1.0 - f) * 6.0
        J[l] = j
        G[l] = RELAX / j

    def right_side(l):
        b = free(l) * HT[l]
        B0[l] = b
        X[l] = G[l] * b

    loop(9, 15, conduct)
    loop(10, 14, faces)
    loop(10, 14, right_side)
    e_design.wait_recv()
    loop(5, 9, conduct)
    loop(15, 19, conduct)

    def pair_z1(n, scale):
        rows = T0[pl.ds(0, n * 48, 2), :] + T0[pl.ds(1, n * 48, 2), :]
        return (exact_dot(rows, TOZ1[...]) * scale).reshape(n, 48, 128)

    def pair_cond(i):
        T0[pl.ds(pl.multiple_of(i * 96, 8), 96), :] = COND[8 + 2 * i] + COND[9 + 2 * i]

    loop(0, 4, pair_cond)
    C1[pl.ds(4, 4)] = pair_z1(4, 0.125)
    CP[0] = C1[4] + pltpu.roll(C1[5], 64, 1)
    CP[1] = C1[6] + pltpu.roll(C1[7], 64, 1)
    e_cond = together([(CP, CR.at[0], block(1)), (CP, CR.at[1], block(-1))], CR)

    def pair_z2(src, msg, scale):
        for i in range(2):
            T1[pl.ds(48 * i, 48), :] = src(2 * i) + src(2 * i + 1)
        rows = T1[pl.ds(0, 48, 2), :] + T1[pl.ds(1, 48, 2), :]
        msg[...] = (exact_dot(rows[:24], TOZ2A[...]) + exact_dot(rows[24:], TOZ2B[...])) * scale


    e_mask.wait_recv()
    loop(6, 10, faces)
    loop(14, 18, faces)
    e_heat.wait_recv()
    loop(6, 10, right_side)
    loop(14, 18, right_side)

    def apply0(ref, l):
        return stencil(ref[l], ref[l - 1], ref[l + 1], CX[l - 1], CX[l], CY[l], CZ[l])

    def sweep0(src, dst, b):
        def one_layer(l):
            dst[l] = src[l] * THIRD + G[l] * (b[l] + apply0(src, l))

        return one_layer

    def residual0(src, b, first):
        def pair(i):
            total = None
            for k in range(2):
                l = first + 2 * i + k
                r = b[l] - J[l] * src[l] + apply0(src, l)
                total = r if total is None else total + r
            T0[pl.ds(pl.multiple_of(i * 96, 8), 96), :] = total

        return pair

    def apply1(ref, l):
        return stencil(ref[l], ref[l - 1], ref[l + 1], CX1[l - 1], CX1[l], CY1[l], CZ1[l])

    def sweep1(src, dst):
        def one_layer(l):
            dst[l] = src[l] * THIRD + G1[l] * (B1[l] + apply1(src, l))

        return one_layer

    def faces1():
        shape = (48, 128)
        lane, row = lanes(shape), rows_of(shape)
        for side, base in ((0, 0), (1, 8)):
            for i in range(2):
                v = CR[side, i]
                C1[base + 2 * i] = jnp.where(lane < 64, v, 0.0)
                C1[base + 2 * i + 1] = jnp.where(lane < 64, pltpu.roll(v, 64, 1), 0.0)
        CX1[0] = C1[0] + C1[1]

        def one_layer(l):
            c = C1[l]
            md, mu = joined(l - 1, 3, 7), joined(l, 3, 7)
            cp = C1[l + 1]
            cyp = jnp.where(row == 47, 0.0, up_y(c))
            czp = up_z(c)
            cym = jnp.where(row == 0, 0.0, dn_y(c))
            czm = dn_z(c)
            CX1[l] = mu * (c + cp)
            CY1[l] = jnp.where(row == 47, 0.0, c + cyp)
            CZ1[l] = jnp.where(lane >= 63, 0.0, c + czp)
            diag = 6.0 * c + (mu * cp + md * C1[l - 1] + (cyp + cym) + (czp + czm))
            j = jnp.where(lane < 64, diag, 1.0)
            J1[l] = j
            G1[l] = RELAX / j

        loop(1, 11, one_layer)

    def level1_down(msg, packed):
        def start(l):
            X1[l] = G1[l] * B1[l]

        loop(2, 10, start, 4)
        loop(3, 9, sweep1(X1, Y1))
        for l in range(4):
            packed[l] = Y1[4 + l] + pltpu.roll(B1[4 + l], 64, 1)

        def mismatch(i):
            l = 4 + i
            return B1[l] - J1[l] * Y1[l] + apply1(Y1, l)

        pair_z2(mismatch, msg, 0.5)

    def level1_up(recv, a):
        for side, base in ((0, 0), (1, 8)):
            for i in range(4):
                v = recv[side, i]
                Y1[base + i] = v
                B1[base + i] = pltpu.roll(v, 64, 1)
        for l in range(a, 12 - a):
            X1[l] = Y1[l] + PT1[(l % 4) // 2, pl.ds(48 * (l // 4), 48), :]
        loop(a + 1, 11 - a, sweep1(X1, Y1))
        loop(a + 2, 10 - a, sweep1(Y1, X1))

    wide = (WIN * 24, 128)
    lane2 = lanes(wide)
    block2 = lax.broadcasted_iota(jnp.int32, (WIN, 24, 128), 0).reshape(wide)
    y2 = lax.broadcasted_iota(jnp.int32, (WIN, 24, 128), 1).reshape(wide)
    cut = lax.rem(NB - 1 - me + REACH, NB)

    def around2(v):
        n = v.shape[0]
        lane = lanes(v.shape)
        plus, minus = pltpu.roll(v, 32, 1), pltpu.roll(v, 96, 1)
        above = jnp.where(lane < 32, minus, pltpu.roll(plus, n - 24, 0))
        below = jnp.where(lane < 32, pltpu.roll(minus, 24, 0), plus)
        return above, below

    def faces2():
        c = C2[...].reshape(wide)
        above, below = around2(c)
        low = lane2 < 32
        used = lane2 < 64
        above = jnp.where((block2 == cut) & (lane2 >= 32), 0.0, above)
        below = jnp.where((block2 == cut + 1) & low, 0.0, below)
        cyp = jnp.where(y2 == 23, 0.0, up_y(c))
        cym = jnp.where(y2 == 0, 0.0, dn_y(c))
        zl = lane2 & 31
        czp = jnp.where(zl == 31, 0.0, up_z(c))
        czm = jnp.where(zl == 0, 0.0, dn_z(c))
        cut_up = ((block2 == cut) & (lane2 >= 32)) | (lane2 >= 64)
        cut_down = ((block2 == cut + 1) & low) | (lane2 >= 64)
        CXU2[...] = jnp.where(cut_up, 0.0, 2.0 * (c + above))
        CXD2[...] = jnp.where(cut_down, 0.0, 2.0 * (c + below))
        CY2[...] = jnp.where(y2 == 23, 0.0, 2.0 * (c + cyp))
        CZ2[...] = jnp.where((zl == 31) | (lane2 >= 64), 0.0, 2.0 * (c + czp))
        diag = 12.0 * c + 2.0 * ((above + below) + (cyp + cym) + (czp + czm))
        j = jnp.where(used, diag, 1.0)
        J2[...] = j
        G2[...] = RELAX / j
        T3[pl.ds(0, 312), :] = exact_dot(c, TOZ3[...])
        c3 = (T3[pl.ds(0, 160, 2), :] + T3[pl.ds(1, 160, 2), :]) * 0.125
        shape = (160, 128)
        lane, row = lanes(shape), rows_of(shape)
        blk = lax.shift_right_logical(row * 5462, 16)
        y = row - 12 * blk
        a3 = jnp.where(blk == cut, 0.0, pltpu.roll(c3, 148, 0))
        b3 = jnp.where(blk == cut + 1, 0.0, pltpu.roll(c3, 12, 0))
        yp = jnp.where(y == 11, 0.0, up_y(c3))
        ym = jnp.where(y == 0, 0.0, dn_y(c3))
        zp, zm = up_z(c3), dn_z(c3)
        CX3[...] = jnp.where(blk == cut, 0.0, 4.0 * (c3 + a3))
        CY3[...] = jnp.where(y == 11, 0.0, 4.0 * (c3 + yp))
        CZ3[...] = jnp.where(lane >= 15, 0.0, 4.0 * (c3 + zp))
        diag3 = 24.0 * c3 + 4.0 * ((a3 + b3) + (yp + ym) + (zp + zm))
        j3 = jnp.where((lane < 16) & (row < 156), diag3, 1.0)
        J3[...] = j3
        G3[...] = RELAX / j3

    def apply2(x, part):
        above, below = around2(x)
        cy, cz = CY2[part, :], CZ2[part, :]
        s = CXU2[part, :] * above + CXD2[part, :] * below
        s = s + (cy * up_y(x) + dn_y(cy * x))
        return s + (cz * up_z(x) + dn_z(cz * x))

    def apply3(x):
        cx, cy, cz = CX3[...], CY3[...], CZ3[...]
        s = cx * pltpu.roll(x, 148, 0) + pltpu.roll(cx * x, 12, 0)
        s = s + (cy * up_y(x) + dn_y(cy * x))
        return s + (cz * up_z(x) + dn_z(cz * x))

    def coarse(buf):
        whole = pl.ds(0, WIN * 24)
        b = buf[...].reshape(wide)
        x = G2[...] * b
        x = x * THIRD + G2[...] * (b + apply2(x, whole))
        X2[...] = x
        r = b - J2[...] * x + apply2(x, whole)
        T3[pl.ds(0, 312), :] = exact_dot(r, TOZ3[...])
        b3 = (T3[pl.ds(0, 160, 2), :] + T3[pl.ds(1, 160, 2), :]) * 0.5
        g3 = G3[...]
        x3 = g3 * b3
        for _ in range(3):
            x3 = x3 * THIRD + g3 * (b3 + apply3(x3))
        spread = exact_dot(x3[48:112], FRZ3[...])
        PT2[pl.ds(0, 64, 2), :] = spread
        PT2[pl.ds(1, 64, 2), :] = spread
        part = pl.ds(96, 120)
        b = buf[pl.ds(4, 5)].reshape(120, 128)
        x = X2[part, :] + PT2[pl.ds(0, 120), :]
        g = G2[part, :]
        for _ in range(2):
            x = x * THIRD + g * (b + apply2(x, part))
        x = x[24:96]
        for k, m in enumerate((FRZ2A, FRZ2B)):
            spread = exact_dot(x, m[...])
            PT1[k, pl.ds(0, 72, 2), :] = spread
            PT1[k, pl.ds(1, 72, 2), :] = spread

    def spread0(first, n):
        x = X1[pl.ds(first, n)].reshape(n * 48, 128)
        spread = exact_dot(x, FRZ1[...])
        PT0[pl.ds(0, n * 48, 2), :] = spread
        PT0[pl.ds(1, n * 48, 2), :] = spread

        def add(i):
            p = PT0[pl.ds(pl.multiple_of(i * 96, 8), 96), :]
            l = 2 * (first + i)
            X[l] = Y[l] + p
            X[l + 1] = Y[l + 1] + p

        loop(0, n, add)

    loop(7, 17, sweep0(X, Y, B0))
    loop(0, 4, residual0(Y, B0, 8), 1)
    B1[pl.ds(4, 4)] = pair_z1(4, 0.5)
    BP[0] = B1[4] + pltpu.roll(B1[5], 64, 1)
    BP[1] = B1[6] + pltpu.roll(B1[7], 64, 1)
    e_b1 = together([(BP.at[1], BR.at[0], block(1)), (BP.at[0], BR.at[1], block(-1))], BR)
    pair_z2(lambda i: C1[4 + i], MC, 0.125)
    g_cond = gather(MC, C2)
    e_next = together(rim(D, 3, 4) + rim(MK, 4, 5) + rim(HT, 5, 6), layers(6))
    e_cond.wait_recv()
    faces1()
    e_b1.wait_recv()
    for side, base in ((0, 2), (1, 8)):
        B1[base] = BR[side]
        B1[base + 1] = pltpu.roll(BR[side], 64, 1)
    level1_down(MG.at[0], MP.at[0])
    g_one = gather(MG.at[0], R.at[0])
    e_m1 = together([(MP.at[0], MR.at[0, 0], block(1)), (MP.at[0], MR.at[0, 1], block(-1))], MR.at[0])

    e_rest = together(rim(D, 0, 3) + rim(MK, 1, 4), layers(12))

    g_cond.wait_recv()
    faces2()

    def slope_factor(l):
        d, weight = density(l)
        DW[l - 8] = (-3.0 * 0.99) * (d * d) / weight

    loop(8, 16, slope_factor)
    e_next.wait_recv()
    for l in (4, 19):
        conduct(l)
    for l in (5, 18):
        faces(l)
    for l in (5, 18):
        right_side(l)
    for l in (6, 17):
        sweep0(X, Y, B0)(l)

    g_one.wait_recv()
    coarse(R.at[0])
    e_m1.wait_recv()
    level1_up(MR.at[0], 1)
    spread0(3, 6)
    loop(7, 17, sweep0(X, Y, B0))
    post = sweep0(Y, Z0, B0)
    loop(8, 16, post)
    e_near = together(rim(Z0, 4, 8), layers(8))
    e_far = together(rim(Z0, 1, 4), layers(6))

    def image(l):
        q = J[l] * Z0[l] - apply0(Z0, l)
        Q0[l] = q
        X[l] = G[l] * q

    loop(9, 15, image)
    e_rest.wait_recv()
    loop(1, 4, conduct, 1)
    loop(20, 23, conduct, 1)
    loop(1, 5, faces)
    loop(19, 22, faces, 1)
    e_near.wait_recv()
    loop(5, 9, image)
    loop(15, 19, image)

    def inner0(i, c):
        l = OWN + i
        z = Z0[l]
        return c[0] + fold(B0[l] * z), c[1] + fold(z * Q0[l])

    nil = jnp.zeros((8, 128), F32)
    ar0 = reduce_start(lax.fori_loop(0, 8, inner0, (nil, nil)), AR.at[0])
    pre = sweep0(X, Y, Q0)
    mismatch0 = residual0(Y, Q0, 4)
    loop(6, 18, pre)
    loop(2, 6, mismatch0, 1)
    e_far.wait_recv()
    loop(2, 5, image, 1)
    loop(19, 22, image, 1)
    loop(3, 6, pre, 1)
    loop(18, 21, pre, 1)
    loop(0, 2, mismatch0, 1)
    loop(6, 8, mismatch0, 1)
    B1[pl.ds(2, 8)] = pair_z1(8, 0.5)
    level1_down(MG.at[1], MP.at[1])
    g_two = gather(MG.at[1], R.at[1])
    e_m2 = together([(MP.at[1], MR.at[1, 0], block(1)), (MP.at[1], MR.at[1, 1], block(-1))], MR.at[1])

    def masked(l):
        VA[l] = free(l) * Z0[l]

    loop(7, 17, masked)
    rho0, pq0 = reduce_done(ar0, AR.at[0], 2)
    a0 = rho0 / pq0
    g_two.wait_recv()
    coarse(R.at[1])
    e_m2.wait_recv()
    level1_up(MR.at[1], 0)
    spread0(2, 8)
    loop(6, 18, sweep0(X, Y, Q0))

    def last_sweep(l):
        w = Y[l] * THIRD + G[l] * (Q0[l] + apply0(Y, l))
        z = Z0[l] - a0 * w
        X[l] = z
        VB[l] = free(l) * z

    loop(7, 17, last_sweep)

    def inner1(i, c):
        l = OWN + i
        z = X[l]
        bz = J[l] * z - apply0(X, l)
        q = Q0[l]
        r = B0[l] - a0 * q
        return c[0] + fold(r * z), c[1] + fold(z * bz), c[2] + fold(z * q)

    ar1 = reduce_start(lax.fori_loop(0, 8, inner1, (nil, nil, nil)), AR.at[1])

    def forms(l):
        md, mu = joined(l - 1), joined(l)
        row, lane = rows_of(plane), lanes(plane)
        a, b = VA[l], VB[l]

        def gaps(ref, v):
            return (
                v - md * ref[l - 1],
                v - mu * ref[l + 1],
                v - jnp.where(row == ROWS - 1, 0.0, up_y(v)),
                v - jnp.where(lane == 127, 0.0, up_z(v)),
            )

        ga, gb = gaps(VA, a), gaps(VB, b)

        def form(g, h, vv):
            dy, dz = g[2] * h[2], g[3] * h[3]
            e = g[0] * h[0] + g[1] * h[1] + dy + dz
            return e + jnp.where(row == 0, vv, dn_y(dy)) + jnp.where(lane == 0, vv, dn_z(dz))

        EA[l - 8] = form(ga, ga, a * a)
        EB[l - 8] = form(ga, gb, a * b)
        EC[l - 8] = form(gb, gb, b * b)

    loop(8, 16, forms, 1)
    rho1, zbz, zq = reduce_done(ar1, AR.at[1], 3)
    beta = rho1 / rho0
    pq1 = zbz + 2.0 * beta * zq + beta * beta * pq0
    a1 = rho1 / pq1
    on_z0 = a0 + a1 * beta
    faa, fab, fbb = 0.5 * on_z0 * on_z0, on_z0 * a1, 0.5 * a1 * a1

    def energy(l):
        EN[l] = faa * EA[l] + fab * EB[l] + fbb * EC[l]

    def quarter(x):
        return pl.ds(pl.multiple_of(24 * x, 8), 24)

    mine = quarter(mx)
    pieces = ((0, 3), (3, 6), (6, 8))
    e_energy, e_slope = [], []
    for first, end in pieces:
        loop(first, end, energy, 1)
        part = pl.ds(first, end - first)
        e_energy.append(
            together(
                [
                    (EN.at[part, quarter(lax.rem(mx + o, NLOAD)), :], RS.at[o - 1, part], load(o))
                    for o in range(1, NLOAD)
                ],
                RS.at[:, part],
            )
        )

    def answer(i):
        temp_out[0, i] = on_z0 * Z0[OWN + i] + a1 * X[OWN + i]

    loop(0, 8, answer)

    def total(l):
        e = EN[l, mine, :] + RS[0, l] + RS[1, l] + RS[2, l]
        GB[l + 1, mine, :] = e * DW[l, mine, :]

    for came, (first, end) in zip(e_energy, pieces):
        came.wait_recv()
        loop(first, end, total, end - first)
        copies = []
        for edge, layer, halo, o in ((0, 1, 9, -1), (8, 8, 0, 1)):
            if edge in (first, end):
                copies += [
                    (GB.at[layer, mine, :], GB.at[halo, mine, :], {**block(o), **load(k)}) for k in range(NLOAD)
                ]
        part = GB.at[pl.ds(first + 1, end - first), mine, :]
        size = T0.at[pl.ds(0, 24 * (len(copies) + 3 * (end - first))), :]
        e_slope.append(together(copies + [(part, part, load(o)) for o in range(1, NLOAD)], size))

    def smooth(i):
        s = joined(i + 7) * GB[i] + joined(i + 8) * GB[i + 2]
        slope_out[i] = blur(GB[i + 1], s)

    done_to = 1
    for came, (first, end) in zip(e_slope, pieces):
        came.wait_recv()
        ready = end if end == 8 else end - 1
        loop(done_to, ready, smooth, 1)
        done_to = ready
    smooth(0)
    for c in sent:
        c.wait_send()


def relay(temp, slope, temp_out, slope_out, sem):
    copies = [
        pltpu.make_async_copy(temp, temp_out, sem.at[0]),
        pltpu.make_async_copy(slope, slope_out, sem.at[1]),
    ]
    for c in copies:
        c.start()
    for c in copies:
        c.wait()


def body(design, free_mask, heat_load):
    v = lambda *s: pltpu.VMEM(s, F32)
    brick = v(24, ROWS, 128)
    level1 = v(12, 48, 128)
    level2 = v(WIN * 24, 128)
    level3 = v(160, 128)
    square = pltpu.VMEM((128, 128), BF16)
    scratch = [
        brick, pltpu.VMEM((24, ROWS, 128), jnp.int32), brick,
        brick, brick, brick, brick, brick, brick, brick, brick, brick, brick, brick,
        brick, brick, v(8, ROWS, 128), v(8, ROWS, 128), v(8, ROWS, 128),
        v(ROWS, 128), v(ROWS, 128), v(8, ROWS, 128), v(768, 128), v(768, 128),
        level1, level1, level1, level1, level1, level1, level1, level1, level1,
        v(96, 128), v(2, 144, 128), v(2, 48, 128), v(2, 2, 48, 128), v(2, 48, 128), v(2, 48, 128),
        v(2, 4, 48, 128), v(2, 2, 4, 48, 128), v(WIN, 24, 128), v(24, 128),
        v(2, WIN, 24, 128), v(2, 24, 128),
        level2, level2, level2, level2, level2, level2, level2, v(320, 128),
        level3, level3, level3, level3, level3, v(128, 128),
        v(2, NB, 1, 128), v(8, ROWS, 128), v(3, 8, 24, 128), v(10, ROWS, 128),
        square, square, square, square, square, square, square, square,
        pltpu.SemaphoreType.DMA((3,)), pltpu.SemaphoreType.DMA((22,)), pltpu.SemaphoreType.DMA((22,)),
    ]
    inside = pl.BlockSpec(memory_space=pltpu.VMEM)
    hbm = pl.BlockSpec(memory_space=pltpu.HBM)
    outs = (jax.ShapeDtypeStruct(heat_load.shape, F32), jax.ShapeDtypeStruct(design.shape, F32))
    temp, slope = pl.pallas_call(
        kernel,
        out_shape=(pltpu.VMEM(heat_load.shape, F32), pltpu.VMEM(design.shape, F32)),
        in_specs=[hbm] * 3,
        out_specs=(inside, inside),
        scratch_shapes=scratch,
        compiler_params=pltpu.CompilerParams(
            collective_id=0, has_side_effects=True, vmem_limit_bytes=62 * 2**20
        ),
    )(design, free_mask, heat_load)
    return pl.pallas_call(
        relay,
        out_shape=outs,
        in_specs=[inside] * 2,
        out_specs=(hbm, hbm),
        scratch_shapes=[pltpu.SemaphoreType.DMA((2,))],
        compiler_params=pltpu.CompilerParams(vmem_limit_bytes=4 * 2**20),
    )(temp, slope)


def solution(mesh):
    return jax.shard_map(
        body,
        mesh=mesh,
        in_specs=(P("blocks", None, None), P("blocks", None, None), P("loads", "blocks", None, None)),
        out_specs=(P("loads", "blocks", None, None), P("blocks", None, None)),
        check_vma=False,
    )
```

```python
import math

import jax
import jax.numpy as jnp
from jax import lax
from jax.experimental import pallas as pl
from jax.experimental.pallas import tpu as pltpu
from jax.sharding import PartitionSpec as P

F32 = jnp.float32
BF16 = jnp.bfloat16
MESH = pl.DeviceIdType.MESH
EDGE = 1.5 - math.sqrt(2.0)
THIRD = 1.0 / 3.0
RELAX = 2.0 / 3.0
NB = 32
NLOAD = 4
ROWS = 96
OWN = 8
REACH = 6
WIN = 2 * REACH + 1


def up_y(v):
    return pltpu.roll(v, v.shape[0] - 1, 0)


def dn_y(v):
    return pltpu.roll(v, 1, 0)


def up_z(v):
    return pltpu.roll(v, 127, 1)


def dn_z(v):
    return pltpu.roll(v, 1, 1)


def lanes(shape):
    return lax.broadcasted_iota(jnp.int32, shape, len(shape) - 1)


def rows_of(shape):
    return lax.broadcasted_iota(jnp.int32, shape, len(shape) - 2)


def exact_dot(x, m):
    hi = x.astype(BF16)
    rest = x - hi.astype(F32)
    mid = rest.astype(BF16)
    d = lambda a: jnp.dot(a, m, preferred_element_type=F32)
    return d(hi) + d(mid)


def stencil(x, xm, xp, cxm, cx, cy, cz):
    s = cx * xp + cxm * xm
    s = s + (cy * up_y(x) + dn_y(cy * x))
    return s + (cz * up_z(x) + dn_z(cz * x))


def loop(a, b, fn, u=0):
    n = b - a
    u = u or next(k for k in (4, 3, 2) if n % k == 0)
    assert n % u == 0

    def step(i, c):
        for k in range(u):
            fn(a + i * u + k)
        return c

    lax.fori_loop(0, n // u, step, 0)


def fold(v):
    return v.reshape(v.shape[0] // 8, 8, 128).sum(axis=0)


def z_sum(f):
    lane = lanes(f.shape)
    return jnp.where(lane == 0, 0.0, dn_z(f)) + jnp.where(lane == 127, 0.0, up_z(f))


def y_sum(f):
    row = rows_of(f.shape)
    last = f.shape[0] - 1
    return jnp.where(row == 0, 0.0, dn_y(f)) + jnp.where(row == last, 0.0, up_y(f))


def blur(f, s):
    h = 0.5 * f + EDGE * s
    zf = z_sum(f)
    return 1.5 * f + 0.5 * s + z_sum(h) + y_sum(h + EDGE * zf)


def kernel(design, mask, heat, temp_out, slope_out, D, MK, HT, COND, CX, CY, CZ, G, J, X, Y, B0, Z0, Q0,
           VA, VB, EA, EB, EC, W0, W1, DW, T0, PT0, C1, CX1, CY1, CZ1, G1, J1, X1, Y1, B1, T1, PT1, CP, CR, BP, BR,
           MP, MR, C2, MC, R, MG, CXU2, CXD2, CY2, CZ2, G2, J2, X2, T3, CX3, CY3, CZ3, G3, J3, PT2,
           AR, EN, RS, GB, TOZ1, TOZ2A, TOZ2B, TOZ3, FRZ1, FRZ2A, FRZ2B, FRZ3, lsem, ssem, rsem):
    me = lax.axis_index("blocks")
    mx = lax.axis_index("loads")

    def block(o):
        return {"blocks": lax.rem(me + o + NB, NB)}

    def load(o):
        return {"loads": lax.rem(mx + o, NLOAD)}

    local = [
        pltpu.make_async_copy(design, D.at[pl.ds(8, 8)], lsem.at[0]),
        pltpu.make_async_copy(mask, MK.at[pl.ds(8, 8)], lsem.at[1]),
        pltpu.make_async_copy(heat.at[0], HT.at[pl.ds(8, 8)], lsem.at[2]),
    ]
    for c in local:
        c.start()

    barrier = pltpu.get_barrier_semaphore()

    def greet(o, c):
        pl.semaphore_signal(barrier, inc=1, device_id=block(o), device_id_type=MESH)
        return c

    lax.fori_loop(1, NB, greet, 0)
    for o in range(1, NLOAD):
        for device in (load(o), {**block(1), **load(o)}, {**block(-1), **load(o)}):
            pl.semaphore_signal(barrier, inc=1, device_id=device, device_id_type=MESH)

    def joined(l, first=7, last=15):
        ends = ((me == 0) & (l == first)) | ((me == NB - 1) & (l == last))
        return jnp.where(ends, 0.0, 1.0).astype(F32)

    def density(l):
        md, mu = joined(l - 1), joined(l)
        weight = W0[...] + (md + mu) * W1[...]
        return blur(D[l], md * D[l - 1] + mu * D[l + 1]) / weight, weight

    def conduct(l):
        d, _ = density(l)
        COND[l] = 0.01 + 0.99 * (d * d * d)

    for c in local:
        c.wait()
    pl.semaphore_wait(barrier, NB - 1 + 3 * (NLOAD - 1))

    sent = []
    count = [0]

    def together(copies, size):
        k = count[0]
        count[0] += 1
        for src, dst, device in copies:
            pltpu.make_async_remote_copy(
                src_ref=src, dst_ref=dst, send_sem=ssem.at[k], recv_sem=rsem.at[k], device_id=device, device_id_type=MESH
            ).start()
        c = pltpu.make_async_remote_copy(
            src_ref=size, dst_ref=size, send_sem=ssem.at[k], recv_sem=rsem.at[k], device_id=block(1), device_id_type=MESH
        )
        sent.append(c)
        return c

    def rim(ref, a, b):
        n = b - a
        return [
            (ref.at[pl.ds(a + 8, n)], ref.at[pl.ds(a, n)], block(1)),
            (ref.at[pl.ds(16 - b, n)], ref.at[pl.ds(24 - b, n)], block(-1)),
        ]

    def layers(n):
        return D.at[pl.ds(0, n)]

    def gather(msg, buf):
        buf[REACH] = msg[...]
        offsets = [s for o in range(1, REACH + 1) for s in (o, -o)]
        return together([(msg, buf.at[REACH - s], block(s)) for s in offsets], buf.at[pl.ds(0, WIN - 1)])

    def reduce_start(values, buf):
        k = count[0]
        count[0] += 1
        lane = lanes((1, 128))
        row = jnp.zeros((1, 128), F32)
        for i, v in enumerate(values):
            row = jnp.where(lane == i, jnp.sum(v), row)
        buf[me] = row

        def send(i, c):
            o = i
            pltpu.make_async_remote_copy(
                src_ref=buf.at[me], dst_ref=buf.at[me], send_sem=ssem.at[k], recv_sem=rsem.at[k],
                device_id=block(o), device_id_type=MESH,
            ).start()
            return c

        lax.fori_loop(1, NB, send, 0)
        c = pltpu.make_async_remote_copy(
            src_ref=buf.at[pl.ds(0, NB - 1)], dst_ref=buf.at[pl.ds(0, NB - 1)], send_sem=ssem.at[k],
            recv_sem=rsem.at[k], device_id=block(1), device_id_type=MESH,
        )
        sent.append(c)
        return c

    def reduce_done(c, buf, n):
        c.wait_recv()
        total = jnp.sum(buf[...], axis=0)
        return [total[:, i : i + 1] for i in range(n)]

    e_design = together(rim(D, 4, 8), layers(8))
    e_mask = together(rim(MK, 5, 8), layers(6))
    e_heat = together(rim(HT, 6, 8), layers(4))

    ii = lax.broadcasted_iota(jnp.int32, (128, 128), 0)
    jj = lax.broadcasted_iota(jnp.int32, (128, 128), 1)
    half_i = lax.shift_right_logical(ii, 1)
    half_j = lax.shift_right_logical(jj, 1)
    put = lambda ref, cond: ref.__setitem__(Ellipsis, jnp.where(cond, 1.0, 0.0).astype(BF16))
    put(TOZ1, half_i == jj)
    put(TOZ2A, (half_i == jj) & (ii < 64))
    put(TOZ2B, (half_i + 32 == jj) & (ii < 64))
    put(TOZ3, (lax.shift_right_logical(ii & 31, 1) == jj) & (ii < 64))
    put(FRZ1, half_j == ii)
    put(FRZ2A, (half_j == ii) & (jj < 64))
    put(FRZ2B, (half_j + 32 == ii) & (jj < 64))
    put(FRZ3, (lax.shift_right_logical(jj & 31, 1) == ii) & (jj < 64))
    plane = (ROWS, 128)
    lane0, row0 = lanes(plane), rows_of(plane)
    one = lambda cond: jnp.where(cond, 1.0, 0.0)
    nz = 2.0 - one(lane0 == 0) - one(lane0 == 127)
    ny = 2.0 - one(row0 == 0) - one(row0 == ROWS - 1)
    W0[...] = 1.5 + 0.5 * (ny + nz) + EDGE * (ny * nz)
    W1[...] = 0.5 + EDGE * (ny + nz)
    T3[pl.ds(312, 8), :] = jnp.zeros((8, 128), F32)
    COND[0] = jnp.zeros(plane, F32)


    def free(l):
        return MK[l].astype(F32)

    def faces(l):
        c = COND[l]
        md, mu = joined(l - 1), joined(l)
        f = free(l)
        cp = COND[l + 1]
        last_row, last_lane = rows_of(plane) == ROWS - 1, lanes(plane) == 127
        first_row, first_lane = rows_of(plane) == 0, lanes(plane) == 0
        cyp = jnp.where(last_row, 0.0, up_y(c))
        czp = jnp.where(last_lane, 0.0, up_z(c))
        cym = jnp.where(first_row, 0.0, dn_y(c))
        czm = jnp.where(first_lane, 0.0, dn_z(c))
        CX[l] = (0.5 * mu) * (c + cp) * (f * free(l + 1))
        CY[l] = jnp.where(last_row, 0.0, 0.5 * (c + cyp) * (f * up_y(f)))
        CZ[l] = jnp.where(last_lane, 0.0, 0.5 * (c + czp) * (f * up_z(f)))
        diag = 3.0 * c + 0.5 * (mu * cp + md * COND[l - 1] + (cyp + cym) + (czp + czm))
        j = f * diag + (1.0 - f) * 6.0
        J[l] = j
        G[l] = RELAX / j

    def right_side(l):
        b = free(l) * HT[l]
        B0[l] = b
        X[l] = G[l] * b

    loop(9, 15, conduct)
    loop(10, 14, faces)
    loop(10, 14, right_side)
    e_design.wait_recv()
    loop(5, 9, conduct)
    loop(15, 19, conduct)

    def pair_z1(n, scale):
        rows = T0[pl.ds(0, n * 48, 2), :] + T0[pl.ds(1, n * 48, 2), :]
        return (exact_dot(rows, TOZ1[...]) * scale).reshape(n, 48, 128)

    def pair_cond(i):
        T0[pl.ds(pl.multiple_of(i * 96, 8), 96), :] = COND[8 + 2 * i] + COND[9 + 2 * i]

    loop(0, 4, pair_cond)
    C1[pl.ds(4, 4)] = pair_z1(4, 0.125)
    CP[0] = C1[4] + pltpu.roll(C1[5], 64, 1)
    CP[1] = C1[6] + pltpu.roll(C1[7], 64, 1)
    e_cond = together([(CP, CR.at[0], block(1)), (CP, CR.at[1], block(-1))], CR)

    def pair_z2(src, msg, scale):
        for i in range(2):
            T1[pl.ds(48 * i, 48), :] = src(2 * i) + src(2 * i + 1)
        rows = T1[pl.ds(0, 48, 2), :] + T1[pl.ds(1, 48, 2), :]
        msg[...] = (exact_dot(rows[:24], TOZ2A[...]) + exact_dot(rows[24:], TOZ2B[...])) * scale


    e_mask.wait_recv()
    loop(6, 10, faces)
    loop(14, 18, faces)
    e_heat.wait_recv()
    loop(6, 10, right_side)
    loop(14, 18, right_side)

    def apply0(ref, l):
        return stencil(ref[l], ref[l - 1], ref[l + 1], CX[l - 1], CX[l], CY[l], CZ[l])

    def sweep0(src, dst, b):
        def one_layer(l):
            dst[l] = src[l] * THIRD + G[l] * (b[l] + apply0(src, l))

        return one_layer

    def residual0(src, b, first):
        def pair(i):
            total = None
            for k in range(2):
                l = first + 2 * i + k
                r = b[l] - J[l] * src[l] + apply0(src, l)
                total = r if total is None else total + r
            T0[pl.ds(pl.multiple_of(i * 96, 8), 96), :] = total

        return pair

    def apply1(ref, l):
        return stencil(ref[l], ref[l - 1], ref[l + 1], CX1[l - 1], CX1[l], CY1[l], CZ1[l])

    def sweep1(src, dst):
        def one_layer(l):
            dst[l] = src[l] * THIRD + G1[l] * (B1[l] + apply1(src, l))

        return one_layer

    def faces1():
        shape = (48, 128)
        lane, row = lanes(shape), rows_of(shape)
        for side, base in ((0, 0), (1, 8)):
            for i in range(2):
                v = CR[side, i]
                C1[base + 2 * i] = jnp.where(lane < 64, v, 0.0)
                C1[base + 2 * i + 1] = jnp.where(lane < 64, pltpu.roll(v, 64, 1), 0.0)
        CX1[0] = C1[0] + C1[1]

        def one_layer(l):
            c = C1[l]
            md, mu = joined(l - 1, 3, 7), joined(l, 3, 7)
            cp = C1[l + 1]
            cyp = jnp.where(row == 47, 0.0, up_y(c))
            czp = up_z(c)
            cym = jnp.where(row == 0, 0.0, dn_y(c))
            czm = dn_z(c)
            CX1[l] = mu * (c + cp)
            CY1[l] = jnp.where(row == 47, 0.0, c + cyp)
            CZ1[l] = jnp.where(lane >= 63, 0.0, c + czp)
            diag = 6.0 * c + (mu * cp + md * C1[l - 1] + (cyp + cym) + (czp + czm))
            j = jnp.where(lane < 64, diag, 1.0)
            J1[l] = j
            G1[l] = RELAX / j

        loop(1, 11, one_layer)

    def level1_down(msg, packed):
        def start(l):
            X1[l] = G1[l] * B1[l]

        loop(2, 10, start, 4)
        loop(3, 9, sweep1(X1, Y1))
        for l in range(4):
            packed[l] = Y1[4 + l] + pltpu.roll(B1[4 + l], 64, 1)

        def mismatch(i):
            l = 4 + i
            return B1[l] - J1[l] * Y1[l] + apply1(Y1, l)

        pair_z2(mismatch, msg, 0.5)

    def level1_up(recv, a):
        for side, base in ((0, 0), (1, 8)):
            for i in range(4):
                v = recv[side, i]
                Y1[base + i] = v
                B1[base + i] = pltpu.roll(v, 64, 1)
        for l in range(a, 12 - a):
            X1[l] = Y1[l] + PT1[(l % 4) // 2, pl.ds(48 * (l // 4), 48), :]
        loop(a + 1, 11 - a, sweep1(X1, Y1))
        loop(a + 2, 10 - a, sweep1(Y1, X1))

    wide = (WIN * 24, 128)
    lane2 = lanes(wide)
    block2 = lax.broadcasted_iota(jnp.int32, (WIN, 24, 128), 0).reshape(wide)
    y2 = lax.broadcasted_iota(jnp.int32, (WIN, 24, 128), 1).reshape(wide)
    cut = lax.rem(NB - 1 - me + REACH, NB)

    def around2(v):
        n = v.shape[0]
        lane = lanes(v.shape)
        plus, minus = pltpu.roll(v, 32, 1), pltpu.roll(v, 96, 1)
        above = jnp.where(lane < 32, minus, pltpu.roll(plus, n - 24, 0))
        below = jnp.where(lane < 32, pltpu.roll(minus, 24, 0), plus)
        return above, below

    def faces2():
        c = C2[...].reshape(wide)
        above, below = around2(c)
        low = lane2 < 32
        used = lane2 < 64
        above = jnp.where((block2 == cut) & (lane2 >= 32), 0.0, above)
        below = jnp.where((block2 == cut + 1) & low, 0.0, below)
        cyp = jnp.where(y2 == 23, 0.0, up_y(c))
        cym = jnp.where(y2 == 0, 0.0, dn_y(c))
        zl = lane2 & 31
        czp = jnp.where(zl == 31, 0.0, up_z(c))
        czm = jnp.where(zl == 0, 0.0, dn_z(c))
        cut_up = ((block2 == cut) & (lane2 >= 32)) | (lane2 >= 64)
        cut_down = ((block2 == cut + 1) & low) | (lane2 >= 64)
        CXU2[...] = jnp.where(cut_up, 0.0, 2.0 * (c + above))
        CXD2[...] = jnp.where(cut_down, 0.0, 2.0 * (c + below))
        CY2[...] = jnp.where(y2 == 23, 0.0, 2.0 * (c + cyp))
        CZ2[...] = jnp.where((zl == 31) | (lane2 >= 64), 0.0, 2.0 * (c + czp))
        diag = 12.0 * c + 2.0 * ((above + below) + (cyp + cym) + (czp + czm))
        j = jnp.where(used, diag, 1.0)
        J2[...] = j
        G2[...] = RELAX / j
        T3[pl.ds(0, 312), :] = exact_dot(c, TOZ3[...])
        c3 = (T3[pl.ds(0, 160, 2), :] + T3[pl.ds(1, 160, 2), :]) * 0.125
        shape = (160, 128)
        lane, row = lanes(shape), rows_of(shape)
        blk = lax.shift_right_logical(row * 5462, 16)
        y = row - 12 * blk
        a3 = jnp.where(blk == cut, 0.0, pltpu.roll(c3, 148, 0))
        b3 = jnp.where(blk == cut + 1, 0.0, pltpu.roll(c3, 12, 0))
        yp = jnp.where(y == 11, 0.0, up_y(c3))
        ym = jnp.where(y == 0, 0.0, dn_y(c3))
        zp, zm = up_z(c3), dn_z(c3)
        CX3[...] = jnp.where(blk == cut, 0.0, 4.0 * (c3 + a3))
        CY3[...] = jnp.where(y == 11, 0.0, 4.0 * (c3 + yp))
        CZ3[...] = jnp.where(lane >= 15, 0.0, 4.0 * (c3 + zp))
        diag3 = 24.0 * c3 + 4.0 * ((a3 + b3) + (yp + ym) + (zp + zm))
        j3 = jnp.where((lane < 16) & (row < 156), diag3, 1.0)
        J3[...] = j3
        G3[...] = RELAX / j3

    def apply2(x, part):
        above, below = around2(x)
        cy, cz = CY2[part, :], CZ2[part, :]
        s = CXU2[part, :] * above + CXD2[part, :] * below
        s = s + (cy * up_y(x) + dn_y(cy * x))
        return s + (cz * up_z(x) + dn_z(cz * x))

    def apply3(x):
        cx, cy, cz = CX3[...], CY3[...], CZ3[...]
        s = cx * pltpu.roll(x, 148, 0) + pltpu.roll(cx * x, 12, 0)
        s = s + (cy * up_y(x) + dn_y(cy * x))
        return s + (cz * up_z(x) + dn_z(cz * x))

    def coarse(buf):
        whole = pl.ds(0, WIN * 24)
        b = buf[...].reshape(wide)
        x = G2[...] * b
        x = x * THIRD + G2[...] * (b + apply2(x, whole))
        X2[...] = x
        r = b - J2[...] * x + apply2(x, whole)
        T3[pl.ds(0, 312), :] = exact_dot(r, TOZ3[...])
        b3 = (T3[pl.ds(0, 160, 2), :] + T3[pl.ds(1, 160, 2), :]) * 0.5
        g3 = G3[...]
        x3 = g3 * b3
        for _ in range(3):
            x3 = x3 * THIRD + g3 * (b3 + apply3(x3))
        spread = exact_dot(x3[48:112], FRZ3[...])
        PT2[pl.ds(0, 64, 2), :] = spread
        PT2[pl.ds(1, 64, 2), :] = spread
        part = pl.ds(96, 120)
        b = buf[pl.ds(4, 5)].reshape(120, 128)
        x = X2[part, :] + PT2[pl.ds(0, 120), :]
        g = G2[part, :]
        for _ in range(2):
            x = x * THIRD + g * (b + apply2(x, part))
        x = x[24:96]
        for k, m in enumerate((FRZ2A, FRZ2B)):
            spread = exact_dot(x, m[...])
            PT1[k, pl.ds(0, 72, 2), :] = spread
            PT1[k, pl.ds(1, 72, 2), :] = spread

    def spread0(first, n):
        x = X1[pl.ds(first, n)].reshape(n * 48, 128)
        spread = exact_dot(x, FRZ1[...])
        PT0[pl.ds(0, n * 48, 2), :] = spread
        PT0[pl.ds(1, n * 48, 2), :] = spread

        def add(i):
            p = PT0[pl.ds(pl.multiple_of(i * 96, 8), 96), :]
            l = 2 * (first + i)
            X[l] = Y[l] + p
            X[l + 1] = Y[l + 1] + p

        loop(0, n, add)

    loop(7, 17, sweep0(X, Y, B0))
    loop(0, 4, residual0(Y, B0, 8), 1)
    B1[pl.ds(4, 4)] = pair_z1(4, 0.5)
    BP[0] = B1[4] + pltpu.roll(B1[5], 64, 1)
    BP[1] = B1[6] + pltpu.roll(B1[7], 64, 1)
    e_b1 = together([(BP.at[1], BR.at[0], block(1)), (BP.at[0], BR.at[1], block(-1))], BR)
    pair_z2(lambda i: C1[4 + i], MC, 0.125)
    g_cond = gather(MC, C2)
    e_next = together(rim(D, 3, 4) + rim(MK, 4, 5) + rim(HT, 5, 6), layers(6))
    e_cond.wait_recv()
    faces1()
    e_b1.wait_recv()
    for side, base in ((0, 2), (1, 8)):
        B1[base] = BR[side]
        B1[base + 1] = pltpu.roll(BR[side], 64, 1)
    level1_down(MG.at[0], MP.at[0])
    g_one = gather(MG.at[0], R.at[0])
    e_m1 = together([(MP.at[0], MR.at[0, 0], block(1)), (MP.at[0], MR.at[0, 1], block(-1))], MR.at[0])

    e_rest = together(rim(D, 0, 3) + rim(MK, 1, 4), layers(12))

    g_cond.wait_recv()
    faces2()

    def slope_factor(l):
        d, weight = density(l)
        DW[l - 8] = (-3.0 * 0.99) * (d * d) / weight

    loop(8, 16, slope_factor)
    e_next.wait_recv()
    for l in (4, 19):
        conduct(l)
    for l in (5, 18):
        faces(l)
    for l in (5, 18):
        right_side(l)
    for l in (6, 17):
        sweep0(X, Y, B0)(l)

    g_one.wait_recv()
    coarse(R.at[0])
    e_m1.wait_recv()
    level1_up(MR.at[0], 1)
    spread0(3, 6)
    loop(7, 17, sweep0(X, Y, B0))
    post = sweep0(Y, Z0, B0)
    loop(8, 16, post)
    e_near = together(rim(Z0, 4, 8), layers(8))
    e_far = together(rim(Z0, 1, 4), layers(6))

    def image(l):
        q = J[l] * Z0[l] - apply0(Z0, l)
        Q0[l] = q
        X[l] = G[l] * q

    loop(9, 15, image)
    e_rest.wait_recv()
    loop(1, 4, conduct, 1)
    loop(20, 23, conduct, 1)
    loop(1, 5, faces)
    loop(19, 22, faces, 1)
    e_near.wait_recv()
    loop(5, 9, image)
    loop(15, 19, image)

    pre = sweep0(X, Y, Q0)
    mismatch0 = residual0(Y, Q0, 4)
    loop(6, 18, pre)
    loop(2, 6, mismatch0, 1)
    e_far.wait_recv()
    loop(2, 5, image, 1)
    loop(19, 22, image, 1)
    loop(3, 6, pre, 1)
    loop(18, 21, pre, 1)
    loop(0, 2, mismatch0, 1)
    loop(6, 8, mismatch0, 1)
    B1[pl.ds(2, 8)] = pair_z1(8, 0.5)
    level1_down(MG.at[1], MP.at[1])
    g_two = gather(MG.at[1], R.at[1])
    e_m2 = together([(MP.at[1], MR.at[1, 0], block(1)), (MP.at[1], MR.at[1, 1], block(-1))], MR.at[1])

    def inner0(i, c):
        l = OWN + i
        z = Z0[l]
        return c[0] + fold(B0[l] * z), c[1] + fold(z * Q0[l])

    nil = jnp.zeros((8, 128), F32)
    ar0 = reduce_start(lax.fori_loop(0, 8, inner0, (nil, nil)), AR.at[0])

    def masked(l):
        VA[l] = free(l) * Z0[l]

    loop(7, 17, masked)
    g_two.wait_recv()
    coarse(R.at[1])
    e_m2.wait_recv()
    level1_up(MR.at[1], 0)
    spread0(2, 8)
    loop(6, 18, sweep0(X, Y, Q0))

    rho0, pq0 = reduce_done(ar0, AR.at[0], 2)
    a0 = rho0 / pq0

    def last_sweep(l):
        w = Y[l] * THIRD + G[l] * (Q0[l] + apply0(Y, l))
        z = Z0[l] - a0 * w
        X[l] = z
        VB[l] = free(l) * z

    loop(7, 17, last_sweep)

    def inner1(i, c):
        l = OWN + i
        z = X[l]
        bz = J[l] * z - apply0(X, l)
        q = Q0[l]
        r = B0[l] - a0 * q
        return c[0] + fold(r * z), c[1] + fold(z * bz), c[2] + fold(z * q)

    ar1 = reduce_start(lax.fori_loop(0, 8, inner1, (nil, nil, nil)), AR.at[1])

    def forms(l):
        md, mu = joined(l - 1), joined(l)
        row, lane = rows_of(plane), lanes(plane)
        a, b = VA[l], VB[l]

        def gaps(ref, v):
            return (
                v - md * ref[l - 1],
                v - mu * ref[l + 1],
                v - jnp.where(row == ROWS - 1, 0.0, up_y(v)),
                v - jnp.where(lane == 127, 0.0, up_z(v)),
            )

        ga, gb = gaps(VA, a), gaps(VB, b)

        def form(g, h, vv):
            dy, dz = g[2] * h[2], g[3] * h[3]
            e = g[0] * h[0] + g[1] * h[1] + dy + dz
            return e + jnp.where(row == 0, vv, dn_y(dy)) + jnp.where(lane == 0, vv, dn_z(dz))

        EA[l - 8] = form(ga, ga, a * a)
        EB[l - 8] = form(ga, gb, a * b)
        EC[l - 8] = form(gb, gb, b * b)

    loop(8, 16, forms, 1)
    rho1, zbz, zq = reduce_done(ar1, AR.at[1], 3)
    beta = rho1 / rho0
    pq1 = zbz + 2.0 * beta * zq + beta * beta * pq0
    a1 = rho1 / pq1
    on_z0 = a0 + a1 * beta
    faa, fab, fbb = 0.5 * on_z0 * on_z0, on_z0 * a1, 0.5 * a1 * a1

    def energy(l):
        EN[l] = faa * EA[l] + fab * EB[l] + fbb * EC[l]

    def quarter(x):
        return pl.ds(pl.multiple_of(24 * x, 8), 24)

    mine = quarter(mx)
    pieces = ((0, 3), (3, 6), (6, 8))
    e_energy, e_slope = [], []
    for first, end in pieces:
        loop(first, end, energy, 1)
        part = pl.ds(first, end - first)
        e_energy.append(
            together(
                [
                    (EN.at[part, quarter(lax.rem(mx + o, NLOAD)), :], RS.at[o - 1, part], load(o))
                    for o in range(1, NLOAD)
                ],
                RS.at[:, part],
            )
        )

    def answer(i):
        temp_out[0, i] = on_z0 * Z0[OWN + i] + a1 * X[OWN + i]

    loop(0, 8, answer)

    def total(l):
        e = EN[l, mine, :] + RS[0, l] + RS[1, l] + RS[2, l]
        GB[l + 1, mine, :] = e * DW[l, mine, :]

    for came, (first, end) in zip(e_energy, pieces):
        came.wait_recv()
        loop(first, end, total, end - first)
        copies = []
        for edge, layer, halo, o in ((0, 1, 9, -1), (8, 8, 0, 1)):
            if edge in (first, end):
                copies += [
                    (GB.at[layer, mine, :], GB.at[halo, mine, :], {**block(o), **load(k)}) for k in range(NLOAD)
                ]
        part = GB.at[pl.ds(first + 1, end - first), mine, :]
        size = T0.at[pl.ds(0, 24 * (len(copies) + 3 * (end - first))), :]
        e_slope.append(together(copies + [(part, part, load(o)) for o in range(1, NLOAD)], size))

    def smooth(i):
        s = joined(i + 7) * GB[i] + joined(i + 8) * GB[i + 2]
        slope_out[i] = blur(GB[i + 1], s)

    done_to = 1
    for came, (first, end) in zip(e_slope, pieces):
        came.wait_recv()
        ready = end if end == 8 else end - 1
        loop(done_to, ready, smooth, 1)
        done_to = ready
    smooth(0)
    for c in sent:
        c.wait_send()


def relay(temp, slope, temp_out, slope_out, sem):
    copies = [
        pltpu.make_async_copy(temp, temp_out, sem.at[0]),
        pltpu.make_async_copy(slope, slope_out, sem.at[1]),
    ]
    for c in copies:
        c.start()
    for c in copies:
        c.wait()


def body(design, free_mask, heat_load):
    v = lambda *s: pltpu.VMEM(s, F32)
    brick = v(24, ROWS, 128)
    level1 = v(12, 48, 128)
    level2 = v(WIN * 24, 128)
    level3 = v(160, 128)
    square = pltpu.VMEM((128, 128), BF16)
    scratch = [
        brick, pltpu.VMEM((24, ROWS, 128), jnp.int32), brick,
        brick, brick, brick, brick, brick, brick, brick, brick, brick, brick, brick,
        brick, brick, v(8, ROWS, 128), v(8, ROWS, 128), v(8, ROWS, 128),
        v(ROWS, 128), v(ROWS, 128), v(8, ROWS, 128), v(768, 128), v(768, 128),
        level1, level1, level1, level1, level1, level1, level1, level1, level1,
        v(96, 128), v(2, 144, 128), v(2, 48, 128), v(2, 2, 48, 128), v(2, 48, 128), v(2, 48, 128),
        v(2, 4, 48, 128), v(2, 2, 4, 48, 128), v(WIN, 24, 128), v(24, 128),
        v(2, WIN, 24, 128), v(2, 24, 128),
        level2, level2, level2, level2, level2, level2, level2, v(320, 128),
        level3, level3, level3, level3, level3, v(128, 128),
        v(2, NB, 1, 128), v(8, ROWS, 128), v(3, 8, 24, 128), v(10, ROWS, 128),
        square, square, square, square, square, square, square, square,
        pltpu.SemaphoreType.DMA((3,)), pltpu.SemaphoreType.DMA((22,)), pltpu.SemaphoreType.DMA((22,)),
    ]
    inside = pl.BlockSpec(memory_space=pltpu.VMEM)
    hbm = pl.BlockSpec(memory_space=pltpu.HBM)
    outs = (jax.ShapeDtypeStruct(heat_load.shape, F32), jax.ShapeDtypeStruct(design.shape, F32))
    temp, slope = pl.pallas_call(
        kernel,
        out_shape=(pltpu.VMEM(heat_load.shape, F32), pltpu.VMEM(design.shape, F32)),
        in_specs=[hbm] * 3,
        out_specs=(inside, inside),
        scratch_shapes=scratch,
        compiler_params=pltpu.CompilerParams(
            collective_id=0, has_side_effects=True, vmem_limit_bytes=62 * 2**20
        ),
    )(design, free_mask, heat_load)
    return pl.pallas_call(
        relay,
        out_shape=outs,
        in_specs=[inside] * 2,
        out_specs=(hbm, hbm),
        scratch_shapes=[pltpu.SemaphoreType.DMA((2,))],
        compiler_params=pltpu.CompilerParams(vmem_limit_bytes=4 * 2**20),
    )(temp, slope)


def solution(mesh):
    return jax.shard_map(
        body,
        mesh=mesh,
        in_specs=(P("blocks", None, None), P("blocks", None, None), P("loads", "blocks", None, None)),
        out_specs=(P("loads", "blocks", None, None), P("blocks", None, None)),
        check_vma=False,
    )
```

```python
import math

import jax
import jax.numpy as jnp
from jax import lax
from jax.experimental import pallas as pl
from jax.experimental.pallas import tpu as pltpu
from jax.sharding import PartitionSpec as P

F32 = jnp.float32
BF16 = jnp.bfloat16
MESH = pl.DeviceIdType.MESH
EDGE = 1.5 - math.sqrt(2.0)
THIRD = 1.0 / 3.0
RELAX = 2.0 / 3.0
NB = 32
NLOAD = 4
ROWS = 96
OWN = 8
REACH = 6
WIN = 2 * REACH + 1


def up_y(v):
    return pltpu.roll(v, v.shape[0] - 1, 0)


def dn_y(v):
    return pltpu.roll(v, 1, 0)


def up_z(v):
    return pltpu.roll(v, 127, 1)


def dn_z(v):
    return pltpu.roll(v, 1, 1)


def lanes(shape):
    return lax.broadcasted_iota(jnp.int32, shape, len(shape) - 1)


def rows_of(shape):
    return lax.broadcasted_iota(jnp.int32, shape, len(shape) - 2)


def exact_dot(x, m):
    hi = x.astype(BF16)
    rest = x - hi.astype(F32)
    mid = rest.astype(BF16)
    d = lambda a: jnp.dot(a, m, preferred_element_type=F32)
    return d(hi) + d(mid)


def stencil(x, xm, xp, cxm, cx, cy, cz):
    s = cx * xp + cxm * xm
    s = s + (cy * up_y(x) + dn_y(cy * x))
    return s + (cz * up_z(x) + dn_z(cz * x))


def loop(a, b, fn, u=0):
    n = b - a
    u = u or next(k for k in (4, 3, 2) if n % k == 0)
    assert n % u == 0

    def step(i, c):
        for k in range(u):
            fn(a + i * u + k)
        return c

    lax.fori_loop(0, n // u, step, 0)


def fold(v):
    return v.reshape(v.shape[0] // 8, 8, 128).sum(axis=0)


def z_sum(f):
    lane = lanes(f.shape)
    return jnp.where(lane == 0, 0.0, dn_z(f)) + jnp.where(lane == 127, 0.0, up_z(f))


def y_sum(f):
    row = rows_of(f.shape)
    last = f.shape[0] - 1
    return jnp.where(row == 0, 0.0, dn_y(f)) + jnp.where(row == last, 0.0, up_y(f))


def blur(f, s):
    h = 0.5 * f + EDGE * s
    zf = z_sum(f)
    return 1.5 * f + 0.5 * s + z_sum(h) + y_sum(h + EDGE * zf)


def kernel(design, mask, heat, temp_out, slope_out, D, MK, HT, COND, CX, CY, CZ, G, J, X, Y, B0, Z0, Q0,
           VA, VB, EA, EB, EC, W0, W1, DW, T0, PT0, C1, CX1, CY1, CZ1, G1, J1, X1, Y1, B1, T1, PT1, CP, CR, BP, BR,
           MP, MR, C2, MC, R, MG, CXU2, CXD2, CY2, CZ2, G2, J2, X2, T3, CX3, CY3, CZ3, G3, J3, PT2,
           AR, EN, RS, GB, TOZ1, TOZ2A, TOZ2B, TOZ3, FRZ1, FRZ2A, FRZ2B, FRZ3, lsem, ssem, rsem):
    me = lax.axis_index("blocks")
    mx = lax.axis_index("loads")

    def block(o):
        return {"blocks": lax.rem(me + o + NB, NB)}

    def load(o):
        return {"loads": lax.rem(mx + o, NLOAD)}

    local = [
        pltpu.make_async_copy(design, D.at[pl.ds(8, 8)], lsem.at[0]),
        pltpu.make_async_copy(mask, MK.at[pl.ds(8, 8)], lsem.at[1]),
        pltpu.make_async_copy(heat.at[0], HT.at[pl.ds(8, 8)], lsem.at[2]),
    ]
    for c in local:
        c.start()

    barrier = pltpu.get_barrier_semaphore()

    def greet(o, c):
        pl.semaphore_signal(barrier, inc=1, device_id=block(o), device_id_type=MESH)
        return c

    lax.fori_loop(1, NB, greet, 0)
    for o in range(1, NLOAD):
        for device in (load(o), {**block(1), **load(o)}, {**block(-1), **load(o)}):
            pl.semaphore_signal(barrier, inc=1, device_id=device, device_id_type=MESH)

    def joined(l, first=7, last=15):
        ends = ((me == 0) & (l == first)) | ((me == NB - 1) & (l == last))
        return jnp.where(ends, 0.0, 1.0).astype(F32)

    def density(l):
        md, mu = joined(l - 1), joined(l)
        weight = W0[...] + (md + mu) * W1[...]
        return blur(D[l], md * D[l - 1] + mu * D[l + 1]) / weight, weight

    def conduct(l):
        d, _ = density(l)
        COND[l] = 0.01 + 0.99 * (d * d * d)

    for c in local:
        c.wait()
    pl.semaphore_wait(barrier, NB - 1 + 3 * (NLOAD - 1))

    sent = []
    count = [0]

    def together(copies, size):
        k = count[0]
        count[0] += 1
        for src, dst, device in copies:
            pltpu.make_async_remote_copy(
                src_ref=src, dst_ref=dst, send_sem=ssem.at[k], recv_sem=rsem.at[k], device_id=device, device_id_type=MESH
            ).start()
        c = pltpu.make_async_remote_copy(
            src_ref=size, dst_ref=size, send_sem=ssem.at[k], recv_sem=rsem.at[k], device_id=block(1), device_id_type=MESH
        )
        sent.append(c)
        return c

    def rim(ref, a, b):
        n = b - a
        return [
            (ref.at[pl.ds(a + 8, n)], ref.at[pl.ds(a, n)], block(1)),
            (ref.at[pl.ds(16 - b, n)], ref.at[pl.ds(24 - b, n)], block(-1)),
        ]

    def layers(n):
        return D.at[pl.ds(0, n)]

    def gather(msg, buf):
        buf[REACH] = msg[...]
        offsets = [s for o in range(1, REACH + 1) for s in (o, -o)]
        return together([(msg, buf.at[REACH - s], block(s)) for s in offsets], buf.at[pl.ds(0, WIN - 1)])

    def reduce_start(values, buf):
        k = count[0]
        count[0] += 1
        lane = lanes((1, 128))
        row = jnp.zeros((1, 128), F32)
        for i, v in enumerate(values):
            row = jnp.where(lane == i, jnp.sum(v, axis=(0, 1), keepdims=True), row)
        buf[me] = row

        def send(i, c):
            o = i
            pltpu.make_async_remote_copy(
                src_ref=buf.at[me], dst_ref=buf.at[me], send_sem=ssem.at[k], recv_sem=rsem.at[k],
                device_id=block(o), device_id_type=MESH,
            ).start()
            return c

        lax.fori_loop(1, NB, send, 0)
        c = pltpu.make_async_remote_copy(
            src_ref=buf.at[pl.ds(0, NB - 1)], dst_ref=buf.at[pl.ds(0, NB - 1)], send_sem=ssem.at[k],
            recv_sem=rsem.at[k], device_id=block(1), device_id_type=MESH,
        )
        sent.append(c)
        return c

    def reduce_done(c, buf, n):
        c.wait_recv()
        total = jnp.sum(buf[...], axis=0)
        return [total[:, i : i + 1] for i in range(n)]

    e_design = together(rim(D, 4, 8), layers(8))
    e_mask = together(rim(MK, 5, 8), layers(6))
    e_heat = together(rim(HT, 6, 8), layers(4))

    ii = lax.broadcasted_iota(jnp.int32, (128, 128), 0)
    jj = lax.broadcasted_iota(jnp.int32, (128, 128), 1)
    half_i = lax.shift_right_logical(ii, 1)
    half_j = lax.shift_right_logical(jj, 1)
    put = lambda ref, cond: ref.__setitem__(Ellipsis, jnp.where(cond, 1.0, 0.0).astype(BF16))
    put(TOZ1, half_i == jj)
    put(TOZ2A, (half_i == jj) & (ii < 64))
    put(TOZ2B, (half_i + 32 == jj) & (ii < 64))
    put(TOZ3, (lax.shift_right_logical(ii & 31, 1) == jj) & (ii < 64))
    put(FRZ1, half_j == ii)
    put(FRZ2A, (half_j == ii) & (jj < 64))
    put(FRZ2B, (half_j + 32 == ii) & (jj < 64))
    put(FRZ3, (lax.shift_right_logical(jj & 31, 1) == ii) & (jj < 64))
    plane = (ROWS, 128)
    lane0, row0 = lanes(plane), rows_of(plane)
    one = lambda cond: jnp.where(cond, 1.0, 0.0)
    nz = 2.0 - one(lane0 == 0) - one(lane0 == 127)
    ny = 2.0 - one(row0 == 0) - one(row0 == ROWS - 1)
    W0[...] = 1.5 + 0.5 * (ny + nz) + EDGE * (ny * nz)
    W1[...] = 0.5 + EDGE * (ny + nz)
    T3[pl.ds(312, 8), :] = jnp.zeros((8, 128), F32)
    COND[0] = jnp.zeros(plane, F32)


    def free(l):
        return MK[l].astype(F32)

    def faces(l):
        c = COND[l]
        md, mu = joined(l - 1), joined(l)
        f = free(l)
        cp = COND[l + 1]
        last_row, last_lane = rows_of(plane) == ROWS - 1, lanes(plane) == 127
        first_row, first_lane = rows_of(plane) == 0, lanes(plane) == 0
        cyp = jnp.where(last_row, 0.0, up_y(c))
        czp = jnp.where(last_lane, 0.0, up_z(c))
        cym = jnp.where(first_row, 0.0, dn_y(c))
        czm = jnp.where(first_lane, 0.0, dn_z(c))
        CX[l] = (0.5 * mu) * (c + cp) * (f * free(l + 1))
        CY[l] = jnp.where(last_row, 0.0, 0.5 * (c + cyp) * (f * up_y(f)))
        CZ[l] = jnp.where(last_lane, 0.0, 0.5 * (c + czp) * (f * up_z(f)))
        diag = 3.0 * c + 0.5 * (mu * cp + md * COND[l - 1] + (cyp + cym) + (czp + czm))
        j = f * diag + (1.0 - f) * 6.0
        J[l] = j
        G[l] = RELAX / j

    def right_side(l):
        b = free(l) * HT[l]
        B0[l] = b
        X[l] = G[l] * b

    loop(9, 15, conduct)
    loop(10, 14, faces)
    loop(10, 14, right_side)
    e_design.wait_recv()
    loop(5, 9, conduct)
    loop(15, 19, conduct)

    def pair_z1(n, scale):
        rows = T0[pl.ds(0, n * 48, 2), :] + T0[pl.ds(1, n * 48, 2), :]
        return (exact_dot(rows, TOZ1[...]) * scale).reshape(n, 48, 128)

    def pair_cond(i):
        T0[pl.ds(pl.multiple_of(i * 96, 8), 96), :] = COND[8 + 2 * i] + COND[9 + 2 * i]

    loop(0, 4, pair_cond)
    C1[pl.ds(4, 4)] = pair_z1(4, 0.125)
    CP[0] = C1[4] + pltpu.roll(C1[5], 64, 1)
    CP[1] = C1[6] + pltpu.roll(C1[7], 64, 1)
    e_cond = together([(CP, CR.at[0], block(1)), (CP, CR.at[1], block(-1))], CR)

    def pair_z2(src, msg, scale):
        for i in range(2):
            T1[pl.ds(48 * i, 48), :] = src(2 * i) + src(2 * i + 1)
        rows = T1[pl.ds(0, 48, 2), :] + T1[pl.ds(1, 48, 2), :]
        msg[...] = (exact_dot(rows[:24], TOZ2A[...]) + exact_dot(rows[24:], TOZ2B[...])) * scale


    e_mask.wait_recv()
    loop(6, 10, faces)
    loop(14, 18, faces)
    e_heat.wait_recv()
    loop(6, 10, right_side)
    loop(14, 18, right_side)

    def apply0(ref, l):
        return stencil(ref[l], ref[l - 1], ref[l + 1], CX[l - 1], CX[l], CY[l], CZ[l])

    def sweep0(src, dst, b):
        def one_layer(l):
            dst[l] = src[l] * THIRD + G[l] * (b[l] + apply0(src, l))

        return one_layer

    def residual0(src, b, first):
        def pair(i):
            total = None
            for k in range(2):
                l = first + 2 * i + k
                r = b[l] - J[l] * src[l] + apply0(src, l)
                total = r if total is None else total + r
            T0[pl.ds(pl.multiple_of(i * 96, 8), 96), :] = total

        return pair

    def apply1(ref, l):
        return stencil(ref[l], ref[l - 1], ref[l + 1], CX1[l - 1], CX1[l], CY1[l], CZ1[l])

    def sweep1(src, dst):
        def one_layer(l):
            dst[l] = src[l] * THIRD + G1[l] * (B1[l] + apply1(src, l))

        return one_layer

    def faces1():
        shape = (48, 128)
        lane, row = lanes(shape), rows_of(shape)
        for side, base in ((0, 0), (1, 8)):
            for i in range(2):
                v = CR[side, i]
                C1[base + 2 * i] = jnp.where(lane < 64, v, 0.0)
                C1[base + 2 * i + 1] = jnp.where(lane < 64, pltpu.roll(v, 64, 1), 0.0)
        CX1[0] = C1[0] + C1[1]

        def one_layer(l):
            c = C1[l]
            md, mu = joined(l - 1, 3, 7), joined(l, 3, 7)
            cp = C1[l + 1]
            cyp = jnp.where(row == 47, 0.0, up_y(c))
            czp = up_z(c)
            cym = jnp.where(row == 0, 0.0, dn_y(c))
            czm = dn_z(c)
            CX1[l] = mu * (c + cp)
            CY1[l] = jnp.where(row == 47, 0.0, c + cyp)
            CZ1[l] = jnp.where(lane >= 63, 0.0, c + czp)
            diag = 6.0 * c + (mu * cp + md * C1[l - 1] + (cyp + cym) + (czp + czm))
            j = jnp.where(lane < 64, diag, 1.0)
            J1[l] = j
            G1[l] = RELAX / j

        loop(1, 11, one_layer)

    def level1_down(msg):
        def start(l):
            X1[l] = G1[l] * B1[l]

        loop(2, 10, start, 4)
        loop(3, 9, sweep1(X1, Y1))

        def mismatch(i):
            l = 4 + i
            return B1[l] - J1[l] * Y1[l] + apply1(Y1, l)

        pair_z2(mismatch, msg, 0.5)

    def level1_up(recv, a):
        for side, base in ((0, 0), (1, 8)):
            for i in range(4):
                v = recv[side, i]
                Y1[base + i] = v
                B1[base + i] = pltpu.roll(v, 64, 1)
        for l in range(a, 12 - a):
            X1[l] = Y1[l] + PT1[(l % 4) // 2, pl.ds(48 * (l // 4), 48), :]
        loop(a + 1, 11 - a, sweep1(X1, Y1))
        loop(a + 2, 10 - a, sweep1(Y1, X1))

    wide = (WIN * 24, 128)
    lane2 = lanes(wide)
    block2 = lax.broadcasted_iota(jnp.int32, (WIN, 24, 128), 0).reshape(wide)
    y2 = lax.broadcasted_iota(jnp.int32, (WIN, 24, 128), 1).reshape(wide)
    cut = lax.rem(NB - 1 - me + REACH, NB)

    def around2(v):
        n = v.shape[0]
        lane = lanes(v.shape)
        plus, minus = pltpu.roll(v, 32, 1), pltpu.roll(v, 96, 1)
        above = jnp.where(lane < 32, minus, pltpu.roll(plus, n - 24, 0))
        below = jnp.where(lane < 32, pltpu.roll(minus, 24, 0), plus)
        return above, below

    def faces2():
        c = C2[...].reshape(wide)
        above, below = around2(c)
        low = lane2 < 32
        used = lane2 < 64
        above = jnp.where((block2 == cut) & (lane2 >= 32), 0.0, above)
        below = jnp.where((block2 == cut + 1) & low, 0.0, below)
        cyp = jnp.where(y2 == 23, 0.0, up_y(c))
        cym = jnp.where(y2 == 0, 0.0, dn_y(c))
        zl = lane2 & 31
        czp = jnp.where(zl == 31, 0.0, up_z(c))
        czm = jnp.where(zl == 0, 0.0, dn_z(c))
        cut_up = ((block2 == cut) & (lane2 >= 32)) | (lane2 >= 64)
        cut_down = ((block2 == cut + 1) & low) | (lane2 >= 64)
        CXU2[...] = jnp.where(cut_up, 0.0, 2.0 * (c + above))
        CXD2[...] = jnp.where(cut_down, 0.0, 2.0 * (c + below))
        CY2[...] = jnp.where(y2 == 23, 0.0, 2.0 * (c + cyp))
        CZ2[...] = jnp.where((zl == 31) | (lane2 >= 64), 0.0, 2.0 * (c + czp))
        diag = 12.0 * c + 2.0 * ((above + below) + (cyp + cym) + (czp + czm))
        j = jnp.where(used, diag, 1.0)
        J2[...] = j
        G2[...] = RELAX / j
        T3[pl.ds(0, 312), :] = exact_dot(c, TOZ3[...])
        c3 = (T3[pl.ds(0, 160, 2), :] + T3[pl.ds(1, 160, 2), :]) * 0.125
        shape = (160, 128)
        lane, row = lanes(shape), rows_of(shape)
        blk = lax.shift_right_logical(row * 5462, 16)
        y = row - 12 * blk
        a3 = jnp.where(blk == cut, 0.0, pltpu.roll(c3, 148, 0))
        b3 = jnp.where(blk == cut + 1, 0.0, pltpu.roll(c3, 12, 0))
        yp = jnp.where(y == 11, 0.0, up_y(c3))
        ym = jnp.where(y == 0, 0.0, dn_y(c3))
        zp, zm = up_z(c3), dn_z(c3)
        CX3[...] = jnp.where(blk == cut, 0.0, 4.0 * (c3 + a3))
        CY3[...] = jnp.where(y == 11, 0.0, 4.0 * (c3 + yp))
        CZ3[...] = jnp.where(lane >= 15, 0.0, 4.0 * (c3 + zp))
        diag3 = 24.0 * c3 + 4.0 * ((a3 + b3) + (yp + ym) + (zp + zm))
        j3 = jnp.where((lane < 16) & (row < 156), diag3, 1.0)
        J3[...] = j3
        G3[...] = RELAX / j3

    def apply2(x, part):
        above, below = around2(x)
        cy, cz = CY2[part, :], CZ2[part, :]
        s = CXU2[part, :] * above + CXD2[part, :] * below
        s = s + (cy * up_y(x) + dn_y(cy * x))
        return s + (cz * up_z(x) + dn_z(cz * x))

    def apply3(x):
        cx, cy, cz = CX3[...], CY3[...], CZ3[...]
        s = cx * pltpu.roll(x, 148, 0) + pltpu.roll(cx * x, 12, 0)
        s = s + (cy * up_y(x) + dn_y(cy * x))
        return s + (cz * up_z(x) + dn_z(cz * x))

    def coarse(buf):
        whole = pl.ds(0, WIN * 24)
        b = buf[...].reshape(wide)
        x = G2[...] * b
        x = x * THIRD + G2[...] * (b + apply2(x, whole))
        X2[...] = x
        r = b - J2[...] * x + apply2(x, whole)
        T3[pl.ds(0, 312), :] = exact_dot(r, TOZ3[...])
        b3 = (T3[pl.ds(0, 160, 2), :] + T3[pl.ds(1, 160, 2), :]) * 0.5
        g3 = G3[...]
        x3 = g3 * b3
        for _ in range(3):
            x3 = x3 * THIRD + g3 * (b3 + apply3(x3))
        spread = exact_dot(x3[48:112], FRZ3[...])
        PT2[pl.ds(0, 64, 2), :] = spread
        PT2[pl.ds(1, 64, 2), :] = spread
        part = pl.ds(96, 120)
        b = buf[pl.ds(4, 5)].reshape(120, 128)
        x = X2[part, :] + PT2[pl.ds(0, 120), :]
        g = G2[part, :]
        for _ in range(2):
            x = x * THIRD + g * (b + apply2(x, part))
        x = x[24:96]
        for k, m in enumerate((FRZ2A, FRZ2B)):
            spread = exact_dot(x, m[...])
            PT1[k, pl.ds(0, 72, 2), :] = spread
            PT1[k, pl.ds(1, 72, 2), :] = spread

    def spread0(first, n):
        x = X1[pl.ds(first, n)].reshape(n * 48, 128)
        spread = exact_dot(x, FRZ1[...])
        PT0[pl.ds(0, n * 48, 2), :] = spread
        PT0[pl.ds(1, n * 48, 2), :] = spread

        def add(i):
            p = PT0[pl.ds(pl.multiple_of(i * 96, 8), 96), :]
            l = 2 * (first + i)
            X[l] = Y[l] + p
            X[l + 1] = Y[l + 1] + p

        loop(0, n, add)

    loop(7, 17, sweep0(X, Y, B0))
    loop(0, 4, residual0(Y, B0, 8), 1)
    B1[pl.ds(4, 4)] = pair_z1(4, 0.5)
    BP[0] = B1[4] + pltpu.roll(B1[5], 64, 1)
    BP[1] = B1[6] + pltpu.roll(B1[7], 64, 1)
    e_b1 = together([(BP.at[1], BR.at[0], block(1)), (BP.at[0], BR.at[1], block(-1))], BR)
    pair_z2(lambda i: C1[4 + i], MC, 0.125)
    g_cond = gather(MC, C2)
    e_next = together(rim(D, 3, 4) + rim(MK, 4, 5) + rim(HT, 5, 6), layers(6))
    e_cond.wait_recv()
    faces1()
    e_b1.wait_recv()
    for side, base in ((0, 2), (1, 8)):
        B1[base] = BR[side]
        B1[base + 1] = pltpu.roll(BR[side], 64, 1)
    level1_down(MG.at[0])
    g_one = gather(MG.at[0], R.at[0])
    for l in range(4):
        MP[0, l] = Y1[4 + l] + pltpu.roll(B1[4 + l], 64, 1)
    e_m1 = together([(MP.at[0], MR.at[0, 0], block(1)), (MP.at[0], MR.at[0, 1], block(-1))], MR.at[0])

    e_rest = together(rim(D, 0, 3) + rim(MK, 1, 4), layers(12))

    g_cond.wait_recv()
    faces2()

    def slope_factor(l):
        d, weight = density(l)
        DW[l - 8] = (-3.0 * 0.99) * (d * d) / weight

    loop(8, 16, slope_factor)
    e_next.wait_recv()
    for l in (4, 19):
        conduct(l)
    for l in (5, 18):
        faces(l)
    for l in (5, 18):
        right_side(l)
    for l in (6, 17):
        sweep0(X, Y, B0)(l)

    g_one.wait_recv()
    coarse(R.at[0])
    e_m1.wait_recv()
    level1_up(MR.at[0], 1)
    spread0(3, 6)
    loop(7, 17, sweep0(X, Y, B0))
    post = sweep0(Y, Z0, B0)
    loop(8, 16, post)
    e_near = together(rim(Z0, 4, 8), layers(8))
    e_far = together(rim(Z0, 1, 4), layers(6))

    def image(l):
        q = J[l] * Z0[l] - apply0(Z0, l)
        Q0[l] = q
        X[l] = G[l] * q

    loop(9, 15, image)
    e_rest.wait_recv()
    loop(1, 4, conduct, 1)
    loop(20, 23, conduct, 1)
    loop(1, 5, faces)
    loop(19, 22, faces, 1)
    e_near.wait_recv()
    loop(5, 9, image)
    loop(15, 19, image)

    pre = sweep0(X, Y, Q0)
    mismatch0 = residual0(Y, Q0, 4)
    loop(6, 18, pre)
    loop(2, 6, mismatch0, 1)
    e_far.wait_recv()
    loop(2, 5, image, 1)
    loop(19, 22, image, 1)
    loop(3, 6, pre, 1)
    loop(18, 21, pre, 1)
    loop(0, 2, mismatch0, 1)
    loop(6, 8, mismatch0, 1)
    B1[pl.ds(2, 8)] = pair_z1(8, 0.5)
    level1_down(MG.at[1])
    g_two = gather(MG.at[1], R.at[1])
    for l in range(4):
        MP[1, l] = Y1[4 + l] + pltpu.roll(B1[4 + l], 64, 1)
    e_m2 = together([(MP.at[1], MR.at[1, 0], block(1)), (MP.at[1], MR.at[1, 1], block(-1))], MR.at[1])

    def inner0(i, c):
        l = OWN + i
        z = Z0[l]
        return c[0] + fold(B0[l] * z), c[1] + fold(z * Q0[l])

    nil = jnp.zeros((8, 128), F32)
    ar0 = reduce_start(lax.fori_loop(0, 8, inner0, (nil, nil)), AR.at[0])

    def masked(l):
        VA[l] = free(l) * Z0[l]

    loop(7, 17, masked)
    g_two.wait_recv()
    coarse(R.at[1])
    e_m2.wait_recv()
    level1_up(MR.at[1], 0)
    spread0(2, 8)
    loop(6, 18, sweep0(X, Y, Q0))

    rho0, pq0 = reduce_done(ar0, AR.at[0], 2)
    a0 = rho0 / pq0

    def last_sweep(l):
        w = Y[l] * THIRD + G[l] * (Q0[l] + apply0(Y, l))
        z = Z0[l] - a0 * w
        X[l] = z
        VB[l] = free(l) * z

    loop(7, 17, last_sweep)

    def inner1(i, c):
        l = OWN + i
        z = X[l]
        bz = J[l] * z - apply0(X, l)
        q = Q0[l]
        r = B0[l] - a0 * q
        return c[0] + fold(r * z), c[1] + fold(z * bz), c[2] + fold(z * q)

    ar1 = reduce_start(lax.fori_loop(0, 8, inner1, (nil, nil, nil)), AR.at[1])

    def forms(l):
        md, mu = joined(l - 1), joined(l)
        row, lane = rows_of(plane), lanes(plane)
        a, b = VA[l], VB[l]

        def gaps(ref, v):
            return (
                v - md * ref[l - 1],
                v - mu * ref[l + 1],
                v - jnp.where(row == ROWS - 1, 0.0, up_y(v)),
                v - jnp.where(lane == 127, 0.0, up_z(v)),
            )

        ga, gb = gaps(VA, a), gaps(VB, b)

        def form(g, h, vv):
            dy, dz = g[2] * h[2], g[3] * h[3]
            e = g[0] * h[0] + g[1] * h[1] + dy + dz
            return e + jnp.where(row == 0, vv, dn_y(dy)) + jnp.where(lane == 0, vv, dn_z(dz))

        EA[l - 8] = form(ga, ga, a * a)
        EB[l - 8] = form(ga, gb, a * b)
        EC[l - 8] = form(gb, gb, b * b)

    loop(8, 16, forms, 1)
    rho1, zbz, zq = reduce_done(ar1, AR.at[1], 3)
    beta = rho1 / rho0
    pq1 = zbz + 2.0 * beta * zq + beta * beta * pq0
    a1 = rho1 / pq1
    on_z0 = a0 + a1 * beta
    faa, fab, fbb = 0.5 * on_z0 * on_z0, on_z0 * a1, 0.5 * a1 * a1

    def energy(l):
        EN[l] = faa * EA[l] + fab * EB[l] + fbb * EC[l]

    def quarter(x):
        return pl.ds(pl.multiple_of(24 * x, 8), 24)

    mine = quarter(mx)
    pieces = ((0, 3), (3, 6), (6, 8))
    e_energy, e_slope = [], []
    for first, end in pieces:
        loop(first, end, energy, 1)
        part = pl.ds(first, end - first)
        e_energy.append(
            together(
                [
                    (EN.at[part, quarter(lax.rem(mx + o, NLOAD)), :], RS.at[o - 1, part], load(o))
                    for o in range(1, NLOAD)
                ],
                RS.at[:, part],
            )
        )

    def answer(i):
        temp_out[0, i] = on_z0 * Z0[OWN + i] + a1 * X[OWN + i]

    loop(0, 8, answer)

    def total(l):
        e = EN[l, mine, :] + RS[0, l] + RS[1, l] + RS[2, l]
        GB[l + 1, mine, :] = e * DW[l, mine, :]

    for came, (first, end) in zip(e_energy, pieces):
        came.wait_recv()
        loop(first, end, total, end - first)
        copies = []
        for edge, layer, halo, o in ((0, 1, 9, -1), (8, 8, 0, 1)):
            if edge in (first, end):
                copies += [
                    (GB.at[layer, mine, :], GB.at[halo, mine, :], {**block(o), **load(k)}) for k in range(NLOAD)
                ]
        part = GB.at[pl.ds(first + 1, end - first), mine, :]
        size = T0.at[pl.ds(0, 24 * (len(copies) + 3 * (end - first))), :]
        e_slope.append(together(copies + [(part, part, load(o)) for o in range(1, NLOAD)], size))

    def smooth(i):
        s = joined(i + 7) * GB[i] + joined(i + 8) * GB[i + 2]
        slope_out[i] = blur(GB[i + 1], s)

    done_to = 1
    for came, (first, end) in zip(e_slope, pieces):
        came.wait_recv()
        ready = end if end == 8 else end - 1
        loop(done_to, ready, smooth, 1)
        done_to = ready
    smooth(0)
    for c in sent:
        c.wait_send()


def relay(temp, slope, temp_out, slope_out, sem):
    copies = [
        pltpu.make_async_copy(temp, temp_out, sem.at[0]),
        pltpu.make_async_copy(slope, slope_out, sem.at[1]),
    ]
    for c in copies:
        c.start()
    for c in copies:
        c.wait()


def body(design, free_mask, heat_load):
    v = lambda *s: pltpu.VMEM(s, F32)
    brick = v(24, ROWS, 128)
    level1 = v(12, 48, 128)
    level2 = v(WIN * 24, 128)
    level3 = v(160, 128)
    square = pltpu.VMEM((128, 128), BF16)
    scratch = [
        brick, pltpu.VMEM((24, ROWS, 128), jnp.int32), brick,
        brick, brick, brick, brick, brick, brick, brick, brick, brick, brick, brick,
        brick, brick, v(8, ROWS, 128), v(8, ROWS, 128), v(8, ROWS, 128),
        v(ROWS, 128), v(ROWS, 128), v(8, ROWS, 128), v(768, 128), v(768, 128),
        level1, level1, level1, level1, level1, level1, level1, level1, level1,
        v(96, 128), v(2, 144, 128), v(2, 48, 128), v(2, 2, 48, 128), v(2, 48, 128), v(2, 48, 128),
        v(2, 4, 48, 128), v(2, 2, 4, 48, 128), v(WIN, 24, 128), v(24, 128),
        v(2, WIN, 24, 128), v(2, 24, 128),
        level2, level2, level2, level2, level2, level2, level2, v(320, 128),
        level3, level3, level3, level3, level3, v(128, 128),
        v(2, NB, 1, 128), v(8, ROWS, 128), v(3, 8, 24, 128), v(10, ROWS, 128),
        square, square, square, square, square, square, square, square,
        pltpu.SemaphoreType.DMA((3,)), pltpu.SemaphoreType.DMA((22,)), pltpu.SemaphoreType.DMA((22,)),
    ]
    inside = pl.BlockSpec(memory_space=pltpu.VMEM)
    hbm = pl.BlockSpec(memory_space=pltpu.HBM)
    outs = (jax.ShapeDtypeStruct(heat_load.shape, F32), jax.ShapeDtypeStruct(design.shape, F32))
    temp, slope = pl.pallas_call(
        kernel,
        out_shape=(pltpu.VMEM(heat_load.shape, F32), pltpu.VMEM(design.shape, F32)),
        in_specs=[hbm] * 3,
        out_specs=(inside, inside),
        scratch_shapes=scratch,
        compiler_params=pltpu.CompilerParams(
            collective_id=0, has_side_effects=True, vmem_limit_bytes=62 * 2**20
        ),
    )(design, free_mask, heat_load)
    return pl.pallas_call(
        relay,
        out_shape=outs,
        in_specs=[inside] * 2,
        out_specs=(hbm, hbm),
        scratch_shapes=[pltpu.SemaphoreType.DMA((2,))],
        compiler_params=pltpu.CompilerParams(vmem_limit_bytes=4 * 2**20),
    )(temp, slope)


def solution(mesh):
    return jax.shard_map(
        body,
        mesh=mesh,
        in_specs=(P("blocks", None, None), P("blocks", None, None), P("loads", "blocks", None, None)),
        out_specs=(P("loads", "blocks", None, None), P("blocks", None, None)),
        check_vma=False,
    )
```
